512 devices in a mesh: seq: 64 (over z, x_hi, core), head: 8 (over y, x_lo).
Axes of the slice: x: 4 (x_hi: 2, x_lo: 2; x = x_hi * 2 + x_lo), y: 4, z: 16, core: 2. Of those that a mesh axis runs over, the one named last changes fastest.
Arguments:
- stream_in: bfloat16 [64, 256, 2048], P('seq', None, 'head'), may hold values from -6 to 6
- row_query: bfloat16 [64, 256, 2048], P('seq', None, 'head'), may hold values from -240 to 240
- row_key: bfloat16 [64, 256, 2048], P('seq', None, 'head'), may hold values from -6 to 6
- row_value: bfloat16 [64, 256, 2048], P('seq', None, 'head'), may hold values from -6 to 6
- out_weight: bfloat16 [2048, 2048], P('head'), may hold values from -0.1875 to 0.1875
- norm_gain: float32 [2048], replicated, may hold values from 0.1 to 1.9
- qkv_weight: bfloat16 [2048, 3, 2048], P('seq', None, 'head'), may hold values from -5 to 5
Outputs:
- stream_out: bfloat16 [64, 256, 2048], P('seq', None, 'head')
- column_mixed: bfloat16 [64, 256, 2048], P('seq', None, 'head')
The draws below stay inside these ranges and needn't reach their ends.
All inputs are finite; a program needn't handle non-finite values.
Results may differ from the reference program's by a relative error of at most 0.01295.
Values may be sent and summed in bfloat16 or wider, within the bound.
No kernel may reach another device: no remote copies, remote signals or barrier semaphores. Data moves between devices by JAX's collectives and lax.ppermute only.
A program may use at most 64 MiB of HBM per device.

```python
import jax
import jax.numpy as jnp
from jax import lax

D = 2048
HEAD = 128
HEADS = 16
C = 256
ROWS = 64


def paired(key, lift):
    keys_raw = jnp.clip(jax.random.normal(jax.random.fold_in(key, 101), (ROWS, C, D), jnp.float32), -6.0, 6.0)
    queries_raw = jnp.clip(jax.random.normal(jax.random.fold_in(key, 102), (ROWS, C, D), jnp.float32), -6.0, 6.0)
    positions = jnp.arange(C)[None, :, None]
    picked = (jax.random.randint(jax.random.fold_in(key, 103), (ROWS, C, 1), 0, 16) == 0) & (positions >= 3)
    chosen = picked.astype(jnp.float32)
    twin = jnp.roll(chosen, -2, axis=1)
    key_matrix_rows = keys_raw * (1.0 - lift * twin)
    query_rows = queries_raw * (1.0 - lift * chosen)
    return (query_rows, key_matrix_rows)


def draw_row_query(key, part):
    lift = 0.0
    query_rows, key_matrix_rows = paired(key, lift)
    return query_rows.astype(jnp.bfloat16)


def draw_row_key(key, part):
    lift = 0.0
    query_rows, key_matrix_rows = paired(key, lift)
    return key_matrix_rows.astype(jnp.bfloat16)


def draw_qkv_weight(key, part):
    key = jax.random.fold_in(key, 7)
    base = jnp.clip(jax.random.normal(jax.random.fold_in(key, 1), (D, 3, D), jnp.float32), -6.0, 6.0) * D ** (-0.5)
    return base.astype(jnp.bfloat16)


def spiked(values, own_key, source, target, parts, factor):
    owner, partner = [(jnp.arange(values.shape[dim]) // (values.shape[dim] // parts)).reshape([-1 if axis == dim else 1 for axis in range(values.ndim)]) for dim in (source, target)]
    chosen = jax.random.permutation(own_key, parts)[partner]
    strong = (owner == chosen) | (owner == (partner + parts // 2) % parts)
    return jnp.where(strong, factor * values, values)


def level_of(key, dims, pieces, smallest, largest):
    def one(position, shards_of):
        draws = jax.random.uniform(jax.random.fold_in(jax.random.fold_in(key, 6), position), (shards_of,), jnp.float32, smallest / len(pieces), largest / len(pieces))
        return jnp.repeat(jnp.exp(draws), dims[position] // shards_of).reshape((-1,) + (1,) * (len(dims) - position - 1))

    level = one(*pieces[0])
    for cut in pieces[1:]:
        level = level * one(*cut)
    return level


def bell_draw(own_key, shape, width, bound, split=(), kind=jnp.bfloat16):
    entries = jax.random.normal(own_key, shape, jnp.float32) * width
    if len(split) > 0:
        entries = level_of(own_key, shape, split, -0.22, 0.18) * entries
    return jnp.clip(entries, min=-bound, max=bound).astype(kind)


def noise_with(own_key, extent, spread, limit, split, heavy, kind=jnp.bfloat16):
    values = spread * jax.random.normal(own_key, extent, jnp.float32)
    if split:
        values = values * level_of(own_key, extent, split, -0.22, 0.18)
    return jnp.clip(spiked(values, jax.random.fold_in(own_key, 3), *heavy), -limit, limit).astype(kind)


def setup_inputs(seed: int = 0) -> dict:
    seeds = jax.random.split(jax.random.key(seed), 8)
    stream_in = bell_draw(seeds[0], (ROWS, C, D), 1.0, 6.0, ((0, 64), (2, 8)))
    row_query = draw_row_query(jax.random.fold_in(seeds[7], 71), 0)
    row_key = draw_row_key(jax.random.fold_in(seeds[7], 71), 0)
    row_value = bell_draw(seeds[3], (ROWS, C, D), 1.0, 6.0, ((0, 64), (2, 8)))
    out_weight = noise_with(seeds[4], (D, D), D ** -0.5, 0.1875, ((0, 8),), (0, 1, 8, 2.0))
    norm_gain = jnp.clip(1.0 + 0.18 * jax.random.normal(seeds[5], (D,), jnp.float32), 0.1, 1.9)
    qkv_weight = draw_qkv_weight(jax.random.fold_in(seeds[7], 71), 0)
    return {"stream_in": stream_in, "row_query": row_query, "row_key": row_key, "row_value": row_value, "out_weight": out_weight, "norm_gain": norm_gain, "qkv_weight": qkv_weight}


def attend(query_rows, key_matrix_rows, value_rows):
    signal_length = query_rows.shape[1]
    logit_scores = jnp.einsum('lcu,lfu->lcf', query_rows.astype(jnp.float32), key_matrix_rows.astype(jnp.float32)) * query_rows.shape[-1] ** (-0.5)
    causal = lax.broadcasted_iota(jnp.int32, (signal_length, signal_length), 0) >= lax.broadcasted_iota(jnp.int32, (signal_length, signal_length), 1)
    logit_scores = jnp.where(causal[None], logit_scores, -1e+30)
    highest = lax.optimization_barrier(jnp.max(logit_scores, axis=-1, keepdims=True))
    attention_weight = jnp.exp(logit_scores - highest)
    attention_weight = (attention_weight / lax.optimization_barrier(jnp.sum(attention_weight, axis=-1, keepdims=True))).astype(jnp.bfloat16)
    return jnp.einsum('nsw,nwg->nsg', attention_weight.astype(jnp.float32), value_rows.astype(jnp.float32)).astype(jnp.bfloat16)

def by_heads(query_rows, key_matrix_rows, value_rows):
    batches, signal_length, _ = query_rows.shape

    def split_heads(array):
        return array.reshape(batches, signal_length, HEADS, HEAD).transpose(2, 0, 1, 3)

    def single(triple):
        return attend(triple[0], triple[1], triple[2])
    mixed = lax.map(single, (split_heads(query_rows), split_heads(key_matrix_rows), split_heads(value_rows)))
    return mixed.transpose(1, 2, 0, 3).reshape(batches, signal_length, D)

def reference(stream_in, row_query, row_key, row_value, out_weight, norm_gain, qkv_weight):
    row_mixed = by_heads(row_query, row_key, row_value)
    partial_value = jnp.dot(row_mixed.reshape(ROWS * C, D), out_weight, preferred_element_type=jnp.float32)
    stream_out = (stream_in.astype(jnp.float32) + partial_value.reshape(ROWS, C, D)).astype(jnp.bfloat16)
    value_rows = stream_out.astype(jnp.float32)
    meansq = lax.optimization_barrier(jnp.sum(value_rows * value_rows, axis=-1, keepdims=True)) / D
    normed = (value_rows * lax.rsqrt(meansq + 1e-05) * norm_gain.astype(jnp.float32)).astype(jnp.bfloat16)
    projected = jnp.dot(normed.reshape(ROWS * C, D), qkv_weight.reshape(D, 3 * D), preferred_element_type=jnp.float32)
    projected = projected.astype(jnp.bfloat16).reshape(ROWS, C, 3, D)
    column_query = projected[:, :, 0].transpose(1, 0, 2)
    column_key = projected[:, :, 1].transpose(1, 0, 2)
    column_value = projected[:, :, 2].transpose(1, 0, 2)
    column_mixed = by_heads(column_query, column_key, column_value).transpose(1, 0, 2)
    return (stream_out, column_mixed)
```

```python
import functools

import jax
import jax.numpy as jnp
from jax import lax
from jax.experimental import pallas as pl
from jax.experimental.pallas import tpu as pltpu
from jax.sharding import Mesh, PartitionSpec as P

HEAD = 128
EPS = 1e-05
NEG = -1e30
SEQ = ("z", "xh", "c")
HD = ("y", "xl")


def softmax_mix(q, k, v, mask):
    s = lax.dot_general(q, k, (((1,), (1,)), ((), ())), preferred_element_type=jnp.float32)
    s = jnp.where(mask, s * (HEAD ** -0.5), NEG)
    p = jnp.exp(s - jnp.max(s, axis=-1, keepdims=True))
    w = (p / jnp.sum(p, axis=-1, keepdims=True)).astype(jnp.bfloat16)
    return jnp.dot(w, v, preferred_element_type=jnp.float32).astype(jnp.bfloat16)


def row_kernel(q_ref, k_ref, v_ref, w_ref, out_ref):
    n = q_ref.shape[0]
    mask = lax.broadcasted_iota(jnp.int32, (n, n), 0) >= lax.broadcasted_iota(jnp.int32, (n, n), 1)
    mixed = []
    for h in range(q_ref.shape[1] // HEAD):
        cols = slice(h * HEAD, (h + 1) * HEAD)
        mixed.append(softmax_mix(q_ref[:, cols], k_ref[:, cols], v_ref[:, cols], mask))
    mixed = jnp.concatenate(mixed, axis=1)
    width = out_ref.shape[2]
    for part in range(out_ref.shape[0]):
        out_ref[part] = jnp.dot(
            mixed, w_ref[:, part * width : (part + 1) * width], preferred_element_type=jnp.float32
        ).astype(jnp.bfloat16)


def row_part(q, k, v, w, heads):
    n, local = q.shape
    width = w.shape[1] // heads
    return pl.pallas_call(
        row_kernel,
        out_shape=jax.ShapeDtypeStruct((heads, n, width), jnp.bfloat16),
        in_specs=[pl.BlockSpec(memory_space=pltpu.VMEM)] * 4,
        out_specs=pl.BlockSpec(memory_space=pltpu.VMEM),
        compiler_params=pltpu.CompilerParams(vmem_limit_bytes=32 * 1024 * 1024),
        cost_estimate=pl.CostEstimate(
            flops=2 * n * local * (n * 2 + w.shape[1]), bytes_accessed=3 * 2**20, transcendentals=2 * n * n
        ),
        name="row_attention",
    )(q, k, v, w)


def column_kernel(where_ref, x_ref, gain_ref, own_ref, other_ref, out_ref, w_ref, normed_ref, sems):
    xh = where_ref[0]
    core = where_ref[1]
    copies = []
    for side, ref in enumerate((own_ref, other_ref)):
        c = core if side == 0 else 1 - core
        for g in range(2):
            x = xh if g == 0 else 1 - xh
            for j in range(3):
                copies.append(
                    pltpu.make_async_copy(ref.at[:, g, j], w_ref.at[j, :, x, c], sems.at[side, g, j])
                )
    for copy in copies:
        copy.start()
    heads, n, local = x_ref.shape
    total = jnp.zeros((n, 1), jnp.float32)
    for h in range(heads):
        x = x_ref[h].astype(jnp.float32)
        total = total + jnp.sum(x * x, axis=1, keepdims=True)
    scale = lax.rsqrt(total / (heads * local) + EPS)
    for h in range(heads):
        cols = slice(h * local, (h + 1) * local)
        normed_ref[:, cols] = (x_ref[h].astype(jnp.float32) * scale * gain_ref[:, cols]).astype(jnp.bfloat16)
    for copy in copies:
        copy.wait()
    parts = []
    for j in range(3):
        w = w_ref[j].reshape(heads * local, local)
        parts.append(
            jnp.dot(normed_ref[...], w, preferred_element_type=jnp.float32).astype(jnp.bfloat16)
        )
    q, k, v = parts
    t0 = lax.broadcasted_iota(jnp.int32, (n, n), 0)
    t1 = lax.broadcasted_iota(jnp.int32, (n, n), 1)
    cols_here = 4
    mask = (t0 >= t1) & ((t0 & (cols_here - 1)) == (t1 & (cols_here - 1)))
    for h in range(local // HEAD):
        cols = slice(h * HEAD, (h + 1) * HEAD)
        out_ref[:, cols] = softmax_mix(q[:, cols], k[:, cols], v[:, cols], mask)


def column_part(where, x, gain, own, other):
    heads, n, local = x.shape
    nz, nx, _, rows, _ = own.shape
    vm = pl.BlockSpec(memory_space=pltpu.VMEM)
    anyspace = pl.BlockSpec(memory_space=pl.ANY)
    return pl.pallas_call(
        column_kernel,
        out_shape=jax.ShapeDtypeStruct((n, local), jnp.bfloat16),
        in_specs=[pl.BlockSpec(memory_space=pltpu.SMEM), vm, vm, anyspace, anyspace],
        out_specs=vm,
        scratch_shapes=[
            pltpu.VMEM((3, nz, nx, 2, rows, local), jnp.bfloat16),
            pltpu.VMEM((n, heads * local), jnp.bfloat16),
            pltpu.SemaphoreType.DMA((2, 2, 3)),
        ],
        compiler_params=pltpu.CompilerParams(vmem_limit_bytes=40 * 1024 * 1024),
        cost_estimate=pl.CostEstimate(
            flops=2 * n * heads * local * 3 * local, bytes_accessed=5 * 2**20, transcendentals=2 * n * n
        ),
        name="column_attention",
    )(where, x, gain, own, other)


def on_device(stream_in, row_query, row_key, row_value, out_weight, norm_gain, qkv_weight):
    _, steps, local = row_query.shape
    heads = norm_gain.shape[0] // local
    seq = 64
    here = steps // seq

    w = jnp.transpose(qkv_weight, (1, 0, 2))
    w2 = lax.ppermute(w, "xh", [(0, 1), (1, 0)])

    partial = row_part(row_query[0], row_key[0], row_value[0], out_weight, heads)

    pair = jnp.stack([w, w2])
    own = lax.all_gather(pair, "z", axis=0)

    parts = lax.all_to_all(partial, HD, 0, 0, tiled=True)
    stream = stream_in[0].astype(jnp.float32) + jnp.sum(parts.astype(jnp.float32), axis=0)
    stream_out = stream.astype(jnp.bfloat16)
    columns = lax.all_to_all(stream_out.reshape(seq, here, local), SEQ, 0, 0, tiled=True)
    columns = columns.reshape(seq * here, local)
    x = lax.all_to_all(jnp.broadcast_to(columns[None], (heads,) + columns.shape), HD, 0, 0, tiled=True)
    own, x = lax.optimization_barrier((own, x))
    other = lax.ppermute(own, "c", [(0, 1), (1, 0)])
    where = jnp.stack([lax.axis_index("xh"), lax.axis_index("c")]).astype(jnp.int32)
    mixed = column_part(where, x, norm_gain.reshape(1, -1), own, other)
    back = lax.all_to_all(mixed.reshape(seq, here, local), SEQ, 0, 0, tiled=True)
    return (stream_out[None], back.reshape(1, steps, local))


def solution(mesh):
    fine = Mesh(mesh.devices.reshape(16, 2, 2, 4, 2), SEQ + HD)
    rows = P(SEQ, None, HD)
    return jax.shard_map(
        on_device,
        mesh=fine,
        in_specs=(rows, rows, rows, rows, P(HD, None), P(), rows),
        out_specs=(rows, rows),
        check_vma=False,
    )
```

```python
import functools

import jax
import jax.numpy as jnp
from jax import lax
from jax.experimental import pallas as pl
from jax.experimental.pallas import tpu as pltpu
from jax.sharding import Mesh, PartitionSpec as P

HEAD = 128
EPS = 1e-05
NEG = -1e30
VMEM_BYTES = 60 * 1024 * 1024
SEQ = ("z", "xh", "c")
HD = ("y", "xl")


def softmax_mix(q, k, v, mask):
    s = lax.dot_general(q, k, (((1,), (1,)), ((), ())), preferred_element_type=jnp.float32)
    s = jnp.where(mask, s * (HEAD ** -0.5), NEG)
    p = jnp.exp(s - jnp.max(s, axis=-1, keepdims=True))
    w = (p / jnp.sum(p, axis=-1, keepdims=True)).astype(jnp.bfloat16)
    return jnp.dot(w, v, preferred_element_type=jnp.float32).astype(jnp.bfloat16)


def row_kernel(q_hbm, k_hbm, v_hbm, w_hbm, out_ref, q_ref, k_ref, v_ref, w_ref, sems):
    copies = [
        pltpu.make_async_copy(src, dst, sems.at[i])
        for i, (src, dst) in enumerate(((q_hbm, q_ref), (k_hbm, k_ref), (v_hbm, v_ref), (w_hbm, w_ref)))
    ]
    for copy in copies:
        copy.start()
    for copy in copies[:3]:
        copy.wait()
    n = q_ref.shape[0]
    mask = lax.broadcasted_iota(jnp.int32, (n, n), 0) >= lax.broadcasted_iota(jnp.int32, (n, n), 1)
    mixed = []
    for h in range(q_ref.shape[1] // HEAD):
        cols = slice(h * HEAD, (h + 1) * HEAD)
        mixed.append(softmax_mix(q_ref[:, cols], k_ref[:, cols], v_ref[:, cols], mask))
    mixed = jnp.concatenate(mixed, axis=1)
    copies[3].wait()
    width = out_ref.shape[2]
    for part in range(out_ref.shape[0]):
        out_ref[part] = jnp.dot(
            mixed, w_ref[:, part * width : (part + 1) * width], preferred_element_type=jnp.float32
        ).astype(jnp.bfloat16)


def row_part(q, k, v, w, heads):
    n, local = q.shape
    width = w.shape[1] // heads
    tile = pltpu.VMEM((n, local), jnp.bfloat16)
    return pl.pallas_call(
        row_kernel,
        out_shape=jax.ShapeDtypeStruct((heads, n, width), jnp.bfloat16),
        in_specs=[pl.BlockSpec(memory_space=pltpu.HBM)] * 4,
        out_specs=pl.BlockSpec(memory_space=pltpu.VMEM),
        scratch_shapes=[tile, tile, tile, pltpu.VMEM(w.shape, jnp.bfloat16), pltpu.SemaphoreType.DMA((4,))],
        compiler_params=pltpu.CompilerParams(vmem_limit_bytes=VMEM_BYTES),
        cost_estimate=pl.CostEstimate(
            flops=2 * n * local * (n * 2 + w.shape[1]), bytes_accessed=3 * 2**20, transcendentals=2 * n * n
        ),
        name="row_attention",
    )(q, k, v, w)


def pack_kernel(count, *refs):
    pieces, out_ref = refs[:count], refs[-1]
    at = 0
    for ref in pieces:
        for i in range(ref.shape[0]):
            out_ref[at + i] = ref[i]
        at += ref.shape[0]


def pack(*pieces, event=()):
    total = sum(p.shape[0] for p in pieces)
    shape = (total,) + pieces[0].shape[1:]
    size = 4
    for d in shape:
        size *= d
    vm = pl.BlockSpec(memory_space=pltpu.VMEM)
    return pl.pallas_call(
        functools.partial(pack_kernel, len(pieces)),
        out_shape=jax.ShapeDtypeStruct(shape, pieces[0].dtype),
        in_specs=[vm] * len(pieces) + [pl.BlockSpec(memory_space=pl.ANY)] * len(event),
        out_specs=vm,
        compiler_params=pltpu.CompilerParams(vmem_limit_bytes=16 * 1024 * 1024),
        cost_estimate=pl.CostEstimate(flops=0, bytes_accessed=size, transcendentals=0),
        name="pack",
    )(*pieces, *event)


FOUR = (0, 4, -4, 8)
SLOTS = (
    [(f, o) for o in (0, 1) for f in FOUR]
    + [(1 + f, o) for o in (0, 1) for f in FOUR]
    + [(-1 + f, o) for o in (0, 1) for f in FOUR]
    + [(2 + f, 0) for f in FOUR]
    + [(-2 + f, 1) for f in FOUR]
)


def column_kernel(where_ref, x_ref, gain_ref, own_ref, other_ref, out_ref, w_ref, normed_ref):
    z, xh, core = where_ref[0], where_ref[1], where_ref[2]
    for side, ref in enumerate((own_ref, other_ref)):
        c = core if side == 0 else 1 - core
        for i, (off, flip) in enumerate(SLOTS):
            zi = lax.rem(z + (off + 16), 16)
            xi = 1 - xh if flip else xh
            for j in range(3):
                w_ref[j, zi, xi, c] = ref[i, j]
    heads, n, local = x_ref.shape
    total = jnp.zeros((n, 1), jnp.float32)
    for h in range(heads):
        x = x_ref[h].astype(jnp.float32)
        total = total + jnp.sum(x * x, axis=1, keepdims=True)
    scale = lax.rsqrt(total / (heads * local) + EPS)
    for h in range(heads):
        cols = slice(h * local, (h + 1) * local)
        normed_ref[:, cols] = (x_ref[h].astype(jnp.float32) * scale * gain_ref[:, cols]).astype(jnp.bfloat16)
    parts = []
    for j in range(3):
        w = w_ref[j].reshape(heads * local, local)
        parts.append(
            jnp.dot(normed_ref[...], w, preferred_element_type=jnp.float32).astype(jnp.bfloat16)
        )
    q, k, v = parts
    t0 = lax.broadcasted_iota(jnp.int32, (n, n), 0)
    t1 = lax.broadcasted_iota(jnp.int32, (n, n), 1)
    cols_here = 4
    mask = (t0 >= t1) & ((t0 & (cols_here - 1)) == (t1 & (cols_here - 1)))
    for h in range(local // HEAD):
        cols = slice(h * HEAD, (h + 1) * HEAD)
        out_ref[:, cols] = softmax_mix(q[:, cols], k[:, cols], v[:, cols], mask)


def column_part(where, x, gain, own, other):
    heads, n, local = x.shape
    rows = own.shape[2]
    vm = pl.BlockSpec(memory_space=pltpu.VMEM)
    return pl.pallas_call(
        column_kernel,
        out_shape=jax.ShapeDtypeStruct((n, local), jnp.bfloat16),
        in_specs=[pl.BlockSpec(memory_space=pltpu.SMEM), vm, vm, vm, vm],
        out_specs=vm,
        scratch_shapes=[
            pltpu.VMEM((3, 16, 2, 2, rows, local), jnp.bfloat16),
            pltpu.VMEM((n, heads * local), jnp.bfloat16),
        ],
        compiler_params=pltpu.CompilerParams(vmem_limit_bytes=40 * 1024 * 1024),
        cost_estimate=pl.CostEstimate(
            flops=2 * n * heads * local * 3 * local, bytes_accessed=5 * 2**20, transcendentals=2 * n * n
        ),
        name="column_attention",
    )(where, x, gain, own, other)


def shift(x, d):
    return lax.ppermute(x, "z", [((i + d) % 16, i) for i in range(16)])


def on_device(stream_in, row_query, row_key, row_value, out_weight, norm_gain, qkv_weight):
    _, steps, local = row_query.shape
    heads = norm_gain.shape[0] // local
    seq = 64
    here = steps // seq

    w = jnp.transpose(qkv_weight, (1, 0, 2))[None]
    fours = [shift(w, d) for d in FOUR[1:]]
    partial = row_part(row_query[0], row_key[0], row_value[0], out_weight, heads)
    parts = lax.all_to_all(partial, HD, 0, 0, tiled=True)
    mine = pack(w, *fours)
    theirs = lax.ppermute(mine, "xh", [(0, 1), (1, 0)])
    stream = stream_in[0].astype(jnp.float32) + jnp.sum(parts.astype(jnp.float32), axis=0)
    stream_out = stream.astype(jnp.bfloat16)
    columns = lax.all_to_all(stream_out.reshape(seq, here, local), SEQ, 0, 0, tiled=True)
    both = pack(mine, theirs, event=(stream_out,))
    up1, down1, up2, down2 = shift(both, 1), shift(both, -1), shift(mine, 2), shift(theirs, -2)
    columns = columns.reshape(seq * here, local)
    x = lax.all_to_all(jnp.broadcast_to(columns[None], (heads,) + columns.shape), HD, 0, 0, tiled=True)
    own = pack(both, up1, down1, up2, down2, event=(columns,))
    other = lax.ppermute(own, "c", [(0, 1), (1, 0)])
    where = jnp.stack([lax.axis_index("z"), lax.axis_index("xh"), lax.axis_index("c")]).astype(jnp.int32)
    mixed = column_part(where, x, norm_gain.reshape(1, -1), own, other)
    back = lax.all_to_all(mixed.reshape(seq, here, local), SEQ, 0, 0, tiled=True)
    return (stream_out[None], back.reshape(1, steps, local))


def solution(mesh):
    fine = Mesh(mesh.devices.reshape(16, 2, 2, 4, 2), SEQ + HD)
    rows = P(SEQ, None, HD)
    return jax.shard_map(
        on_device,
        mesh=fine,
        in_specs=(rows, rows, rows, rows, P(HD, None), P(), rows),
        out_specs=(rows, rows),
        check_vma=False,
    )
```

```python
import functools

import jax
import jax.numpy as jnp
from jax import lax
from jax.experimental import pallas as pl
from jax.experimental.pallas import tpu as pltpu
from jax.sharding import Mesh, PartitionSpec as P

HEAD = 128
EPS = 1e-05
NEG = -1e30
VMEM_BYTES = 60 * 1024 * 1024
SEQ = ("z", "xh", "c")
HD = ("y", "xl")


def softmax_mix(q, k, v, mask):
    s = lax.dot_general(q, k, (((1,), (1,)), ((), ())), preferred_element_type=jnp.float32)
    s = jnp.where(mask, s * (HEAD ** -0.5), NEG)
    p = jnp.exp(s - jnp.max(s, axis=-1, keepdims=True))
    w = (p / jnp.sum(p, axis=-1, keepdims=True)).astype(jnp.bfloat16)
    return jnp.dot(w, v, preferred_element_type=jnp.float32).astype(jnp.bfloat16)


def row_kernel(q_hbm, k_hbm, v_hbm, w_hbm, out_ref, q_ref, k_ref, v_ref, w_ref, sems):
    copies = [
        pltpu.make_async_copy(src, dst, sems.at[i])
        for i, (src, dst) in enumerate(((q_hbm, q_ref), (k_hbm, k_ref), (v_hbm, v_ref), (w_hbm, w_ref)))
    ]
    for copy in copies:
        copy.start()
    for copy in copies[:3]:
        copy.wait()
    n = q_ref.shape[0]
    mask = lax.broadcasted_iota(jnp.int32, (n, n), 0) >= lax.broadcasted_iota(jnp.int32, (n, n), 1)
    mixed = []
    for h in range(q_ref.shape[1] // HEAD):
        cols = slice(h * HEAD, (h + 1) * HEAD)
        mixed.append(softmax_mix(q_ref[:, cols], k_ref[:, cols], v_ref[:, cols], mask))
    mixed = jnp.concatenate(mixed, axis=1)
    copies[3].wait()
    width = out_ref.shape[2]
    for part in range(out_ref.shape[0]):
        out_ref[part] = jnp.dot(
            mixed, w_ref[:, part * width : (part + 1) * width], preferred_element_type=jnp.float32
        ).astype(jnp.bfloat16)


def row_part(q, k, v, w, heads):
    n, local = q.shape
    width = w.shape[1] // heads
    tile = pltpu.VMEM((n, local), jnp.bfloat16)
    return pl.pallas_call(
        row_kernel,
        out_shape=jax.ShapeDtypeStruct((heads, n, width), jnp.bfloat16),
        in_specs=[pl.BlockSpec(memory_space=pltpu.HBM)] * 4,
        out_specs=pl.BlockSpec(memory_space=pltpu.VMEM),
        scratch_shapes=[tile, tile, tile, pltpu.VMEM(w.shape, jnp.bfloat16), pltpu.SemaphoreType.DMA((4,))],
        compiler_params=pltpu.CompilerParams(vmem_limit_bytes=VMEM_BYTES),
        cost_estimate=pl.CostEstimate(
            flops=2 * n * local * (n * 2 + w.shape[1]), bytes_accessed=3 * 2**20, transcendentals=2 * n * n
        ),
        name="row_attention",
    )(q, k, v, w)


def pack_kernel(count, *refs):
    pieces, out_ref = refs[:count], refs[-1]
    at = 0
    for ref in pieces:
        for i in range(ref.shape[0]):
            out_ref[at + i] = ref[i]
        at += ref.shape[0]


def pack(*pieces, event=()):
    total = sum(p.shape[0] for p in pieces)
    shape = (total,) + pieces[0].shape[1:]
    size = 4
    for d in shape:
        size *= d
    vm = pl.BlockSpec(memory_space=pltpu.VMEM)
    return pl.pallas_call(
        functools.partial(pack_kernel, len(pieces)),
        out_shape=jax.ShapeDtypeStruct(shape, pieces[0].dtype),
        in_specs=[vm] * (len(pieces) + len(event)),
        out_specs=vm,
        compiler_params=pltpu.CompilerParams(vmem_limit_bytes=16 * 1024 * 1024),
        cost_estimate=pl.CostEstimate(flops=0, bytes_accessed=size, transcendentals=0),
        name="pack",
    )(*pieces, *event)


FOUR = (0, 4, -4, 8)
EIGHT = [(f, o) for f in FOUR for o in (0, 1)]
SLOTS = (
    EIGHT
    + [(1 + f, o) for f, o in EIGHT]
    + [(-1 + f, o) for f, o in EIGHT]
    + [(2 + f, o) for f, o in EIGHT[:4]]
    + [(-2 + f, o) for f, o in EIGHT[:2] + EIGHT[4:6]]
)


def touch_kernel(x_ref, event_ref, out_ref):
    pass


def touch(x, event):
    anyspace = pl.BlockSpec(memory_space=pl.ANY)
    return pl.pallas_call(
        touch_kernel,
        out_shape=jax.ShapeDtypeStruct(x.shape, x.dtype),
        in_specs=[anyspace, anyspace],
        out_specs=anyspace,
        input_output_aliases={0: 0},
        compiler_params=pltpu.CompilerParams(vmem_limit_bytes=VMEM_BYTES),
        name="touch",
    )(x, event)


def column_kernel(where_ref, x_ref, gain_ref, own_ref, other_ref, out_ref, w_ref, normed_ref):
    z, xh, core = where_ref[0], where_ref[1], where_ref[2]
    for side, ref in enumerate((own_ref, other_ref)):
        c = core if side == 0 else 1 - core
        for i, (off, flip) in enumerate(SLOTS):
            zi = lax.rem(z + (off + 16), 16)
            xi = 1 - xh if flip else xh
            for j in range(3):
                w_ref[j, zi, xi, c] = ref[i, j]
    heads, n, local = x_ref.shape
    total = jnp.zeros((n, 1), jnp.float32)
    for h in range(heads):
        x = x_ref[h].astype(jnp.float32)
        total = total + jnp.sum(x * x, axis=1, keepdims=True)
    scale = lax.rsqrt(total / (heads * local) + EPS)
    for h in range(heads):
        cols = slice(h * local, (h + 1) * local)
        normed_ref[:, cols] = (x_ref[h].astype(jnp.float32) * scale * gain_ref[:, cols]).astype(jnp.bfloat16)
    parts = []
    for j in range(3):
        w = w_ref[j].reshape(heads * local, local)
        parts.append(
            jnp.dot(normed_ref[...], w, preferred_element_type=jnp.float32).astype(jnp.bfloat16)
        )
    q, k, v = parts
    t0 = lax.broadcasted_iota(jnp.int32, (n, n), 0)
    t1 = lax.broadcasted_iota(jnp.int32, (n, n), 1)
    cols_here = 4
    mask = (t0 >= t1) & ((t0 & (cols_here - 1)) == (t1 & (cols_here - 1)))
    for h in range(local // HEAD):
        cols = slice(h * HEAD, (h + 1) * HEAD)
        out_ref[:, cols] = softmax_mix(q[:, cols], k[:, cols], v[:, cols], mask)


def column_part(where, x, gain, own, other):
    heads, n, local = x.shape
    rows = own.shape[2]
    vm = pl.BlockSpec(memory_space=pltpu.VMEM)
    return pl.pallas_call(
        column_kernel,
        out_shape=jax.ShapeDtypeStruct((n, local), jnp.bfloat16),
        in_specs=[pl.BlockSpec(memory_space=pltpu.SMEM), vm, vm, vm, vm],
        out_specs=vm,
        scratch_shapes=[
            pltpu.VMEM((3, 16, 2, 2, rows, local), jnp.bfloat16),
            pltpu.VMEM((n, heads * local), jnp.bfloat16),
        ],
        compiler_params=pltpu.CompilerParams(vmem_limit_bytes=40 * 1024 * 1024),
        cost_estimate=pl.CostEstimate(
            flops=2 * n * heads * local * 3 * local, bytes_accessed=5 * 2**20, transcendentals=2 * n * n
        ),
        name="column_attention",
    )(where, x, gain, own, other)


def shift(x, d):
    return lax.ppermute(x, "z", [((i + d) % 16, i) for i in range(16)])


def on_device(stream_in, row_query, row_key, row_value, out_weight, norm_gain, qkv_weight):
    _, steps, local = row_query.shape
    heads = norm_gain.shape[0] // local
    seq = 64
    here = steps // seq

    w = jnp.transpose(qkv_weight, (1, 0, 2))[None]
    theirs = lax.ppermute(w, "xh", [(0, 1), (1, 0)])
    partial = row_part(row_query[0], row_key[0], row_value[0], out_weight, heads)
    pair = pack(w, theirs)
    parts = lax.all_to_all(touch(partial, pair[1, 0, :16, :128]), HD, 0, 0, tiled=True)
    up4, down4, up8 = shift(pair, 4), shift(pair, -4), shift(pair, 8)
    stream = stream_in[0].astype(jnp.float32) + jnp.sum(parts.astype(jnp.float32), axis=0)
    stream_out = stream.astype(jnp.bfloat16)
    columns = lax.all_to_all(stream_out.reshape(seq, here, local), SEQ, 0, 0, tiled=True)
    eight = pack(pair, up4, down4, up8, event=(stream_out,))
    first, second = pack(pair, up4, event=(stream_out,)), pack(pair, down4, event=(stream_out,))
    up1, down1, up2, down2 = shift(eight, 1), shift(eight, -1), shift(first, 2), shift(second, -2)
    columns = columns.reshape(seq * here, local)
    x = lax.all_to_all(jnp.broadcast_to(columns[None], (heads,) + columns.shape), HD, 0, 0, tiled=True)
    own = pack(eight, up1, down1, up2, down2, event=(columns,))
    other = lax.ppermute(own, "c", [(0, 1), (1, 0)])
    where = jnp.stack([lax.axis_index("z"), lax.axis_index("xh"), lax.axis_index("c")]).astype(jnp.int32)
    mixed = column_part(where, x, norm_gain.reshape(1, -1), own, other)
    back = lax.all_to_all(mixed.reshape(seq, here, local), SEQ, 0, 0, tiled=True)
    return (stream_out[None], back.reshape(1, steps, local))


def solution(mesh):
    fine = Mesh(mesh.devices.reshape(16, 2, 2, 4, 2), SEQ + HD)
    rows = P(SEQ, None, HD)
    return jax.shard_map(
        on_device,
        mesh=fine,
        in_specs=(rows, rows, rows, rows, P(HD, None), P(), rows),
        out_specs=(rows, rows),
        check_vma=False,
    )
```

```python
import functools

import jax
import jax.numpy as jnp
from jax import lax
from jax.experimental import pallas as pl
from jax.experimental.pallas import tpu as pltpu
from jax.sharding import Mesh, PartitionSpec as P

HEAD = 128
EPS = 1e-05
NEG = -1e30
VMEM_BYTES = 60 * 1024 * 1024
SEQ = ("z", "xh", "c")
HD = ("y", "xl")


def softmax_mix(q, k, v, mask):
    s = lax.dot_general(q, k, (((1,), (1,)), ((), ())), preferred_element_type=jnp.float32)
    s = jnp.where(mask, s * (HEAD ** -0.5), NEG)
    p = jnp.exp(s - jnp.max(s, axis=-1, keepdims=True))
    w = (p / jnp.sum(p, axis=-1, keepdims=True)).astype(jnp.bfloat16)
    return jnp.dot(w, v, preferred_element_type=jnp.float32).astype(jnp.bfloat16)


def row_kernel(q_hbm, k_hbm, v_hbm, w_hbm, out_ref, q_ref, k_ref, v_ref, w_ref, sems):
    copies = [
        pltpu.make_async_copy(src, dst, sems.at[i])
        for i, (src, dst) in enumerate(((q_hbm, q_ref), (k_hbm, k_ref), (v_hbm, v_ref), (w_hbm, w_ref)))
    ]
    for copy in copies:
        copy.start()
    for copy in copies[:3]:
        copy.wait()
    n = q_ref.shape[0]
    mask = lax.broadcasted_iota(jnp.int32, (n, n), 0) >= lax.broadcasted_iota(jnp.int32, (n, n), 1)
    mixed = []
    for h in range(q_ref.shape[1] // HEAD):
        cols = slice(h * HEAD, (h + 1) * HEAD)
        mixed.append(softmax_mix(q_ref[:, cols], k_ref[:, cols], v_ref[:, cols], mask))
    mixed = jnp.concatenate(mixed, axis=1)
    copies[3].wait()
    width = out_ref.shape[2]
    for part in range(out_ref.shape[0]):
        out_ref[part] = jnp.dot(
            mixed, w_ref[:, part * width : (part + 1) * width], preferred_element_type=jnp.float32
        ).astype(jnp.bfloat16)


def row_part(q, k, v, w, heads):
    n, local = q.shape
    width = w.shape[1] // heads
    tile = pltpu.VMEM((n, local), jnp.bfloat16)
    return pl.pallas_call(
        row_kernel,
        out_shape=jax.ShapeDtypeStruct((heads, n, width), jnp.bfloat16),
        in_specs=[pl.BlockSpec(memory_space=pltpu.HBM)] * 4,
        out_specs=pl.BlockSpec(memory_space=pltpu.VMEM),
        scratch_shapes=[tile, tile, tile, pltpu.VMEM(w.shape, jnp.bfloat16), pltpu.SemaphoreType.DMA((4,))],
        compiler_params=pltpu.CompilerParams(vmem_limit_bytes=VMEM_BYTES),
        cost_estimate=pl.CostEstimate(
            flops=2 * n * local * (n * 2 + w.shape[1]), bytes_accessed=3 * 2**20, transcendentals=2 * n * n
        ),
        name="row_attention",
    )(q, k, v, w)


def pack_kernel(count, *refs):
    pieces, out_ref = refs[:count], refs[-1]
    at = 0
    for ref in pieces:
        for i in range(ref.shape[0]):
            out_ref[at + i] = ref[i]
        at += ref.shape[0]


def pack(*pieces, event=()):
    total = sum(p.shape[0] for p in pieces)
    shape = (total,) + pieces[0].shape[1:]
    size = 4
    for d in shape:
        size *= d
    vm = pl.BlockSpec(memory_space=pltpu.VMEM)
    return pl.pallas_call(
        functools.partial(pack_kernel, len(pieces)),
        out_shape=jax.ShapeDtypeStruct(shape, pieces[0].dtype),
        in_specs=[vm] * (len(pieces) + len(event)),
        out_specs=vm,
        compiler_params=pltpu.CompilerParams(vmem_limit_bytes=16 * 1024 * 1024),
        cost_estimate=pl.CostEstimate(flops=0, bytes_accessed=size, transcendentals=0),
        name="pack",
    )(*pieces, *event)


FOUR = (0, 8, -4, 4)
EIGHT = [(f, o) for f in FOUR for o in (0, 1)]
SLOTS = (
    EIGHT
    + [(1 + f, o) for f, o in EIGHT]
    + [(-1 + f, o) for f, o in EIGHT]
    + [(2 + f, o) for f in (0, 4) for o in (0, 1)]
    + [(-2 + f, o) for f in (0, -4) for o in (0, 1)]
)


def touch_kernel(x_ref, event_ref, out_ref):
    pass


def touch(x, event):
    anyspace = pl.BlockSpec(memory_space=pl.ANY)
    return pl.pallas_call(
        touch_kernel,
        out_shape=jax.ShapeDtypeStruct(x.shape, x.dtype),
        in_specs=[anyspace, anyspace],
        out_specs=anyspace,
        input_output_aliases={0: 0},
        compiler_params=pltpu.CompilerParams(vmem_limit_bytes=VMEM_BYTES),
        name="touch",
    )(x, event)


def column_kernel(where_ref, x_ref, gain_ref, own_ref, other_ref, out_ref, w_ref, normed_ref):
    z, xh, core = where_ref[0], where_ref[1], where_ref[2]
    for side, ref in enumerate((own_ref, other_ref)):
        c = core if side == 0 else 1 - core
        for i, (off, flip) in enumerate(SLOTS):
            zi = lax.rem(z + (off + 16), 16)
            xi = 1 - xh if flip else xh
            for j in range(3):
                w_ref[j, zi, xi, c] = ref[i, j]
    heads, n, local = x_ref.shape
    total = jnp.zeros((n, 1), jnp.float32)
    for h in range(heads):
        x = x_ref[h].astype(jnp.float32)
        total = total + jnp.sum(x * x, axis=1, keepdims=True)
    scale = lax.rsqrt(total / (heads * local) + EPS)
    for h in range(heads):
        cols = slice(h * local, (h + 1) * local)
        normed_ref[:, cols] = (x_ref[h].astype(jnp.float32) * scale * gain_ref[:, cols]).astype(jnp.bfloat16)
    parts = []
    for j in range(3):
        w = w_ref[j].reshape(heads * local, local)
        parts.append(
            jnp.dot(normed_ref[...], w, preferred_element_type=jnp.float32).astype(jnp.bfloat16)
        )
    q, k, v = parts
    t0 = lax.broadcasted_iota(jnp.int32, (n, n), 0)
    t1 = lax.broadcasted_iota(jnp.int32, (n, n), 1)
    cols_here = 4
    mask = (t0 >= t1) & ((t0 & (cols_here - 1)) == (t1 & (cols_here - 1)))
    for h in range(local // HEAD):
        cols = slice(h * HEAD, (h + 1) * HEAD)
        out_ref[:, cols] = softmax_mix(q[:, cols], k[:, cols], v[:, cols], mask)


def column_part(where, x, gain, own, other):
    heads, n, local = x.shape
    rows = own.shape[2]
    vm = pl.BlockSpec(memory_space=pltpu.VMEM)
    return pl.pallas_call(
        column_kernel,
        out_shape=jax.ShapeDtypeStruct((n, local), jnp.bfloat16),
        in_specs=[pl.BlockSpec(memory_space=pltpu.SMEM), vm, vm, vm, vm],
        out_specs=vm,
        scratch_shapes=[
            pltpu.VMEM((3, 16, 2, 2, rows, local), jnp.bfloat16),
            pltpu.VMEM((n, heads * local), jnp.bfloat16),
        ],
        compiler_params=pltpu.CompilerParams(vmem_limit_bytes=40 * 1024 * 1024),
        cost_estimate=pl.CostEstimate(
            flops=2 * n * heads * local * 3 * local, bytes_accessed=5 * 2**20, transcendentals=2 * n * n
        ),
        name="column_attention",
    )(where, x, gain, own, other)


def shift(x, d):
    return lax.ppermute(x, "z", [((i + d) % 16, i) for i in range(16)])


def on_device(stream_in, row_query, row_key, row_value, out_weight, norm_gain, qkv_weight):
    _, steps, local = row_query.shape
    heads = norm_gain.shape[0] // local
    seq = 64
    here = steps // seq

    w = jnp.transpose(qkv_weight, (1, 0, 2))[None]
    theirs = lax.ppermute(w, "xh", [(0, 1), (1, 0)])
    partial = row_part(row_query[0], row_key[0], row_value[0], out_weight, heads)
    pair = pack(w, theirs)
    parts = lax.all_to_all(touch(partial, pair[1, 0, :16, :128]), HD, 0, 0, tiled=True)
    up8, down4, up4 = shift(pair, 8), shift(pair, -4), shift(pair, 4)
    stream = stream_in[0].astype(jnp.float32) + jnp.sum(parts.astype(jnp.float32), axis=0)
    stream_out = stream.astype(jnp.bfloat16)
    columns = lax.all_to_all(stream_out.reshape(seq, here, local), SEQ, 0, 0, tiled=True)
    eight = pack(pair, up8, down4, up4, event=(stream_out,))
    first, second = pack(pair, up4, event=(stream_out,)), pack(pair, down4, event=(stream_out,))
    up1, down1, up2, down2 = shift(eight, 1), shift(eight, -1), shift(first, 2), shift(second, -2)
    columns = columns.reshape(seq * here, local)
    x = lax.all_to_all(jnp.broadcast_to(columns[None], (heads,) + columns.shape), HD, 0, 0, tiled=True)
    own = pack(eight, up1, down1, up2, down2, event=(columns,))
    other = lax.ppermute(own, "c", [(0, 1), (1, 0)])
    where = jnp.stack([lax.axis_index("z"), lax.axis_index("xh"), lax.axis_index("c")]).astype(jnp.int32)
    mixed = column_part(where, x, norm_gain.reshape(1, -1), own, other)
    back = lax.all_to_all(mixed.reshape(seq, here, local), SEQ, 0, 0, tiled=True)
    return (stream_out[None], back.reshape(1, steps, local))


def solution(mesh):
    fine = Mesh(mesh.devices.reshape(16, 2, 2, 4, 2), SEQ + HD)
    rows = P(SEQ, None, HD)
    return jax.shard_map(
        on_device,
        mesh=fine,
        in_specs=(rows, rows, rows, rows, P(HD, None), P(), rows),
        out_specs=(rows, rows),
        check_vma=False,
    )
```

```python
import functools

import jax
import jax.numpy as jnp
from jax import lax
from jax.experimental import pallas as pl
from jax.experimental.pallas import tpu as pltpu
from jax.sharding import Mesh, PartitionSpec as P

HEAD = 128
EPS = 1e-05
NEG = -1e30
VMEM_BYTES = 60 * 1024 * 1024
SEQ = ("z", "xh", "c")
HD = ("y", "xl")


def softmax_mix(q, k, v, mask):
    s = lax.dot_general(q, k, (((1,), (1,)), ((), ())), preferred_element_type=jnp.float32)
    s = jnp.where(mask, s * (HEAD ** -0.5), NEG)
    p = jnp.exp(s - jnp.max(s, axis=-1, keepdims=True))
    w = (p / jnp.sum(p, axis=-1, keepdims=True)).astype(jnp.bfloat16)
    return jnp.dot(w, v, preferred_element_type=jnp.float32).astype(jnp.bfloat16)


def row_kernel(q_hbm, k_hbm, v_hbm, w_hbm, out_ref, q_ref, k_ref, v_ref, w_ref, sems):
    copies = [
        pltpu.make_async_copy(src, dst, sems.at[i])
        for i, (src, dst) in enumerate(((q_hbm, q_ref), (k_hbm, k_ref), (v_hbm, v_ref), (w_hbm, w_ref)))
    ]
    for copy in copies:
        copy.start()
    for copy in copies[:3]:
        copy.wait()
    n = q_ref.shape[0]
    mask = lax.broadcasted_iota(jnp.int32, (n, n), 0) >= lax.broadcasted_iota(jnp.int32, (n, n), 1)
    mixed = []
    for h in range(q_ref.shape[1] // HEAD):
        cols = slice(h * HEAD, (h + 1) * HEAD)
        mixed.append(softmax_mix(q_ref[:, cols], k_ref[:, cols], v_ref[:, cols], mask))
    mixed = jnp.concatenate(mixed, axis=1)
    copies[3].wait()
    width = out_ref.shape[2]
    for part in range(out_ref.shape[0]):
        out_ref[part] = jnp.dot(
            mixed, w_ref[:, part * width : (part + 1) * width], preferred_element_type=jnp.float32
        ).astype(jnp.bfloat16)


def row_part(q, k, v, w, heads):
    n, local = q.shape
    width = w.shape[1] // heads
    tile = pltpu.VMEM((n, local), jnp.bfloat16)
    return pl.pallas_call(
        row_kernel,
        out_shape=jax.ShapeDtypeStruct((heads, n, width), jnp.bfloat16),
        in_specs=[pl.BlockSpec(memory_space=pltpu.HBM)] * 4,
        out_specs=pl.BlockSpec(memory_space=pltpu.VMEM),
        scratch_shapes=[tile, tile, tile, pltpu.VMEM(w.shape, jnp.bfloat16), pltpu.SemaphoreType.DMA((4,))],
        compiler_params=pltpu.CompilerParams(vmem_limit_bytes=VMEM_BYTES),
        cost_estimate=pl.CostEstimate(
            flops=2 * n * local * (n * 2 + w.shape[1]), bytes_accessed=3 * 2**20, transcendentals=2 * n * n
        ),
        name="row_attention",
    )(q, k, v, w)


def pack_kernel(count, *refs):
    pieces, out_ref = refs[:count], refs[-1]
    at = 0
    for ref in pieces:
        for i in range(ref.shape[0]):
            out_ref[at + i] = ref[i]
        at += ref.shape[0]


def pack(*pieces, event=(), weight=0):
    total = sum(p.shape[0] for p in pieces)
    shape = (total,) + pieces[0].shape[1:]
    size = 4
    for d in shape:
        size *= d
    vm = pl.BlockSpec(memory_space=pltpu.VMEM)
    return pl.pallas_call(
        functools.partial(pack_kernel, len(pieces)),
        out_shape=jax.ShapeDtypeStruct(shape, pieces[0].dtype),
        in_specs=[vm] * (len(pieces) + len(event)),
        out_specs=vm,
        compiler_params=pltpu.CompilerParams(vmem_limit_bytes=4 * 1024 * 1024),
        cost_estimate=pl.CostEstimate(flops=weight, bytes_accessed=size, transcendentals=0),
        name="pack",
    )(*pieces, *event)


FOUR = (0, 8, -4, 4)
EIGHT = [(f, o) for f in FOUR for o in (0, 1)]
SLOTS = (
    EIGHT
    + [(1 + f, o) for f, o in EIGHT]
    + [(-1 + f, o) for f, o in EIGHT]
    + [(2 + f, o) for f in (0, 4) for o in (0, 1)]
    + [(-2 + f, o) for f in (0, -4) for o in (0, 1)]
)


def touch_kernel(x_ref, event_ref, out_ref):
    pass


def touch(x, event):
    anyspace = pl.BlockSpec(memory_space=pl.ANY)
    return pl.pallas_call(
        touch_kernel,
        out_shape=jax.ShapeDtypeStruct(x.shape, x.dtype),
        in_specs=[anyspace, anyspace],
        out_specs=anyspace,
        input_output_aliases={0: 0},
        compiler_params=pltpu.CompilerParams(vmem_limit_bytes=VMEM_BYTES),
        name="touch",
    )(x, event)


def column_kernel(count, where_ref, x_ref, gain_ref, *refs):
    pieces, (out_ref, w_ref, normed_ref) = refs[: 2 * count], refs[2 * count :]
    z, xh, core = where_ref[0], where_ref[1], where_ref[2]
    for side in (0, 1):
        c = core if side == 0 else 1 - core
        slots = iter(SLOTS)
        for ref in pieces[side * count : (side + 1) * count]:
            for i in range(ref.shape[0]):
                off, flip = next(slots)
                zi = lax.rem(z + (off + 16), 16)
                xi = 1 - xh if flip else xh
                for j in range(3):
                    w_ref[j, zi, xi, c] = ref[i, j]
    heads, n, local = x_ref.shape
    total = jnp.zeros((n, 1), jnp.float32)
    for h in range(heads):
        x = x_ref[h].astype(jnp.float32)
        total = total + jnp.sum(x * x, axis=1, keepdims=True)
    scale = lax.rsqrt(total / (heads * local) + EPS)
    for h in range(heads):
        cols = slice(h * local, (h + 1) * local)
        normed_ref[:, cols] = (x_ref[h].astype(jnp.float32) * scale * gain_ref[:, cols]).astype(jnp.bfloat16)
    parts = []
    for j in range(3):
        w = w_ref[j].reshape(heads * local, local)
        parts.append(
            jnp.dot(normed_ref[...], w, preferred_element_type=jnp.float32).astype(jnp.bfloat16)
        )
    q, k, v = parts
    t0 = lax.broadcasted_iota(jnp.int32, (n, n), 0)
    t1 = lax.broadcasted_iota(jnp.int32, (n, n), 1)
    cols_here = 4
    mask = (t0 >= t1) & ((t0 & (cols_here - 1)) == (t1 & (cols_here - 1)))
    for h in range(local // HEAD):
        cols = slice(h * HEAD, (h + 1) * HEAD)
        out_ref[:, cols] = softmax_mix(q[:, cols], k[:, cols], v[:, cols], mask)


def column_part(where, x, gain, own, other):
    count = len(own)
    heads, n, local = x.shape
    rows = own[0].shape[2]
    vm = pl.BlockSpec(memory_space=pltpu.VMEM)
    return pl.pallas_call(
        functools.partial(column_kernel, count),
        out_shape=jax.ShapeDtypeStruct((n, local), jnp.bfloat16),
        in_specs=[pl.BlockSpec(memory_space=pltpu.SMEM)] + [vm] * (2 + 2 * count),
        out_specs=vm,
        scratch_shapes=[
            pltpu.VMEM((3, 16, 2, 2, rows, local), jnp.bfloat16),
            pltpu.VMEM((n, heads * local), jnp.bfloat16),
        ],
        compiler_params=pltpu.CompilerParams(vmem_limit_bytes=20 * 1024 * 1024),
        cost_estimate=pl.CostEstimate(
            flops=2 * n * heads * local * 3 * local, bytes_accessed=5 * 2**20, transcendentals=2 * n * n
        ),
        name="column_attention",
    )(where, x, gain, *own, *other)


def shift(x, d):
    return lax.ppermute(x, "z", [((i + d) % 16, i) for i in range(16)])


def on_device(stream_in, row_query, row_key, row_value, out_weight, norm_gain, qkv_weight):
    _, steps, local = row_query.shape
    heads = norm_gain.shape[0] // local
    seq = 64
    here = steps // seq

    w = jnp.transpose(qkv_weight, (1, 0, 2))[None]
    theirs = lax.ppermute(w, "xh", [(0, 1), (1, 0)])
    partial = row_part(row_query[0], row_key[0], row_value[0], out_weight, heads)
    pair = pack(w, theirs)
    parts = lax.all_to_all(touch(partial, pair[1, 0, :16, :128]), HD, 0, 0, tiled=True)
    up8, down4, up4 = shift(pair, 8), shift(pair, -4), shift(pair, 4)
    stream = stream_in[0].astype(jnp.float32) + jnp.sum(parts.astype(jnp.float32), axis=0)
    stream_out = stream.astype(jnp.bfloat16)
    columns = lax.all_to_all(stream_out.reshape(seq, here, local), SEQ, 0, 0, tiled=True)
    eight = pack(pair, up8, down4, up4, event=(stream_out,), weight=1000000000)
    first, second = pack(pair, up4, event=(stream_out,)), pack(pair, down4, event=(stream_out,))
    up1, down1, up2, down2 = shift(eight, 1), shift(eight, -1), shift(first, 2), shift(second, -2)
    columns = columns.reshape(seq * here, local)
    x = lax.all_to_all(jnp.broadcast_to(columns[None], (heads,) + columns.shape), HD, 0, 0, tiled=True)
    own = (pack(eight, up1), pack(down1, up2, down2))
    other = [lax.ppermute(piece, "c", [(0, 1), (1, 0)]) for piece in own]
    where = jnp.stack([lax.axis_index("z"), lax.axis_index("xh"), lax.axis_index("c")]).astype(jnp.int32)
    mixed = column_part(where, x, norm_gain.reshape(1, -1), own, other)
    back = lax.all_to_all(mixed.reshape(seq, here, local), SEQ, 0, 0, tiled=True)
    return (stream_out[None], back.reshape(1, steps, local))


def solution(mesh):
    fine = Mesh(mesh.devices.reshape(16, 2, 2, 4, 2), SEQ + HD)
    rows = P(SEQ, None, HD)
    return jax.shard_map(
        on_device,
        mesh=fine,
        in_specs=(rows, rows, rows, rows, P(HD, None), P(), rows),
        out_specs=(rows, rows),
        check_vma=False,
    )
```

```python
import functools

import jax
import jax.numpy as jnp
from jax import lax
from jax.experimental import pallas as pl
from jax.experimental.pallas import tpu as pltpu
from jax.sharding import Mesh, PartitionSpec as P

HEAD = 128
EPS = 1e-05
NEG = -1e30
VMEM_BYTES = 60 * 1024 * 1024
SEQ = ("z", "xh", "c")
HD = ("y", "xl")


def softmax_mix(q, k, v, mask):
    s = lax.dot_general(q, k, (((1,), (1,)), ((), ())), preferred_element_type=jnp.float32)
    s = jnp.where(mask, s * (HEAD ** -0.5), NEG)
    p = jnp.exp(s - jnp.max(s, axis=-1, keepdims=True))
    w = (p / jnp.sum(p, axis=-1, keepdims=True)).astype(jnp.bfloat16)
    return jnp.dot(w, v, preferred_element_type=jnp.float32).astype(jnp.bfloat16)


def row_kernel(q_hbm, k_hbm, v_hbm, w_hbm, out_ref, q_ref, k_ref, v_ref, w_ref, sems):
    copies = [
        pltpu.make_async_copy(src, dst, sems.at[i])
        for i, (src, dst) in enumerate(((q_hbm, q_ref), (k_hbm, k_ref), (v_hbm, v_ref), (w_hbm, w_ref)))
    ]
    for copy in copies:
        copy.start()
    for copy in copies[:3]:
        copy.wait()
    n = q_ref.shape[0]
    mask = lax.broadcasted_iota(jnp.int32, (n, n), 0) >= lax.broadcasted_iota(jnp.int32, (n, n), 1)
    mixed = []
    for h in range(q_ref.shape[1] // HEAD):
        cols = slice(h * HEAD, (h + 1) * HEAD)
        mixed.append(softmax_mix(q_ref[:, cols], k_ref[:, cols], v_ref[:, cols], mask))
    mixed = jnp.concatenate(mixed, axis=1)
    copies[3].wait()
    width = out_ref.shape[2]
    for part in range(out_ref.shape[0]):
        out_ref[part] = jnp.dot(
            mixed, w_ref[:, part * width : (part + 1) * width], preferred_element_type=jnp.float32
        ).astype(jnp.bfloat16)


def row_part(q, k, v, w, heads):
    n, local = q.shape
    width = w.shape[1] // heads
    tile = pltpu.VMEM((n, local), jnp.bfloat16)
    return pl.pallas_call(
        row_kernel,
        out_shape=jax.ShapeDtypeStruct((heads, n, width), jnp.bfloat16),
        in_specs=[pl.BlockSpec(memory_space=pltpu.HBM)] * 4,
        out_specs=pl.BlockSpec(memory_space=pltpu.VMEM),
        scratch_shapes=[tile, tile, tile, pltpu.VMEM(w.shape, jnp.bfloat16), pltpu.SemaphoreType.DMA((4,))],
        compiler_params=pltpu.CompilerParams(vmem_limit_bytes=VMEM_BYTES),
        cost_estimate=pl.CostEstimate(
            flops=2 * n * local * (n * 2 + w.shape[1]), bytes_accessed=3 * 2**20, transcendentals=2 * n * n
        ),
        name="row_attention",
    )(q, k, v, w)


def pack_kernel(*refs):
    pieces, out_ref = refs[:-1], refs[-1]
    at = 0
    for ref in pieces:
        for i in range(ref.shape[0]):
            out_ref[at + i] = ref[i]
        at += ref.shape[0]


def pack(*pieces, weight=0):
    total = sum(p.shape[0] for p in pieces)
    shape = (total,) + pieces[0].shape[1:]
    size = 4
    for d in shape:
        size *= d
    vm = pl.BlockSpec(memory_space=pltpu.VMEM)
    return pl.pallas_call(
        pack_kernel,
        out_shape=jax.ShapeDtypeStruct(shape, pieces[0].dtype),
        in_specs=[vm] * len(pieces),
        out_specs=vm,
        compiler_params=pltpu.CompilerParams(vmem_limit_bytes=4 * 1024 * 1024),
        cost_estimate=pl.CostEstimate(flops=weight, bytes_accessed=size, transcendentals=0),
        name="pack",
    )(*pieces)


def group_kernel(pair_ref, up8_ref, down4_ref, up4_ref, event_ref, eight_ref, first_ref, second_ref):
    for i, ref in enumerate((pair_ref, up8_ref, down4_ref, up4_ref)):
        for o in (0, 1):
            eight_ref[2 * i + o] = ref[o]
    for o in (0, 1):
        first_ref[o] = pair_ref[o]
        first_ref[2 + o] = up4_ref[o]
        second_ref[o] = pair_ref[o]
        second_ref[2 + o] = down4_ref[o]


def group(pair, up8, down4, up4, event, weight):
    vm = pl.BlockSpec(memory_space=pltpu.VMEM)
    shape = pair.shape[1:]
    return pl.pallas_call(
        group_kernel,
        out_shape=[jax.ShapeDtypeStruct((n,) + shape, pair.dtype) for n in (8, 4, 4)],
        in_specs=[vm] * 5,
        out_specs=[vm] * 3,
        compiler_params=pltpu.CompilerParams(vmem_limit_bytes=4 * 1024 * 1024),
        cost_estimate=pl.CostEstimate(flops=weight, bytes_accessed=16 * pair.size, transcendentals=0),
        name="group",
    )(pair, up8, down4, up4, event)


FOUR = (0, 8, -4, 4)
EIGHT = [(f, o) for f in FOUR for o in (0, 1)]
SLOTS = (
    EIGHT
    + [(1 + f, o) for f, o in EIGHT]
    + [(-1 + f, o) for f, o in EIGHT]
    + [(2 + f, o) for f in (0, 4) for o in (0, 1)]
    + [(-2 + f, o) for f in (0, -4) for o in (0, 1)]
)


def column_kernel(count, where_ref, x_ref, gain_ref, *refs):
    pieces, (out_ref, w_ref, normed_ref) = refs[: 2 * count], refs[2 * count :]
    z, xh, core = where_ref[0], where_ref[1], where_ref[2]
    for side in (0, 1):
        c = core if side == 0 else 1 - core
        slots = iter(SLOTS)
        for ref in pieces[side * count : (side + 1) * count]:
            for i in range(ref.shape[0]):
                off, flip = next(slots)
                zi = lax.rem(z + (off + 16), 16)
                xi = 1 - xh if flip else xh
                for j in range(3):
                    w_ref[j, zi, xi, c] = ref[i, j]
    heads, n, local = x_ref.shape
    total = jnp.zeros((n, 1), jnp.float32)
    for h in range(heads):
        x = x_ref[h].astype(jnp.float32)
        total = total + jnp.sum(x * x, axis=1, keepdims=True)
    scale = lax.rsqrt(total / (heads * local) + EPS)
    for h in range(heads):
        cols = slice(h * local, (h + 1) * local)
        normed_ref[:, cols] = (x_ref[h].astype(jnp.float32) * scale * gain_ref[:, cols]).astype(jnp.bfloat16)
    parts = []
    for j in range(3):
        w = w_ref[j].reshape(heads * local, local)
        parts.append(
            jnp.dot(normed_ref[...], w, preferred_element_type=jnp.float32).astype(jnp.bfloat16)
        )
    q, k, v = parts
    t0 = lax.broadcasted_iota(jnp.int32, (n, n), 0)
    t1 = lax.broadcasted_iota(jnp.int32, (n, n), 1)
    cols_here = 4
    mask = (t0 >= t1) & ((t0 & (cols_here - 1)) == (t1 & (cols_here - 1)))
    for h in range(local // HEAD):
        cols = slice(h * HEAD, (h + 1) * HEAD)
        out_ref[:, cols] = softmax_mix(q[:, cols], k[:, cols], v[:, cols], mask)


def column_part(where, x, gain, own, other):
    count = len(own)
    heads, n, local = x.shape
    rows = own[0].shape[2]
    vm = pl.BlockSpec(memory_space=pltpu.VMEM)
    return pl.pallas_call(
        functools.partial(column_kernel, count),
        out_shape=jax.ShapeDtypeStruct((n, local), jnp.bfloat16),
        in_specs=[pl.BlockSpec(memory_space=pltpu.SMEM)] + [vm] * (2 + 2 * count),
        out_specs=vm,
        scratch_shapes=[
            pltpu.VMEM((3, 16, 2, 2, rows, local), jnp.bfloat16),
            pltpu.VMEM((n, heads * local), jnp.bfloat16),
        ],
        compiler_params=pltpu.CompilerParams(vmem_limit_bytes=20 * 1024 * 1024),
        cost_estimate=pl.CostEstimate(
            flops=2 * n * heads * local * 3 * local, bytes_accessed=5 * 2**20, transcendentals=2 * n * n
        ),
        name="column_attention",
    )(where, x, gain, *own, *other)


def shift(x, d):
    return lax.ppermute(x, "z", [((i + d) % 16, i) for i in range(16)])


def on_device(stream_in, row_query, row_key, row_value, out_weight, norm_gain, qkv_weight):
    _, steps, local = row_query.shape
    heads = norm_gain.shape[0] // local
    seq = 64
    here = steps // seq

    w = jnp.transpose(qkv_weight, (1, 0, 2))[None]
    theirs = lax.ppermute(w, "xh", [(0, 1), (1, 0)])
    partial = row_part(row_query[0], row_key[0], row_value[0], out_weight, heads)
    pair = pack(w, theirs, weight=10**10)
    parts = lax.all_to_all(partial, HD, 0, 0, tiled=True)
    up8, down4, up4 = shift(pair, 8), shift(pair, -4), shift(pair, 4)
    stream = stream_in[0].astype(jnp.float32) + jnp.sum(parts.astype(jnp.float32), axis=0)
    stream_out = stream.astype(jnp.bfloat16)
    columns = lax.all_to_all(stream_out.reshape(seq, here, local), SEQ, 0, 0, tiled=True)
    eight, first, second = group(pair, up8, down4, up4, stream_out, 10**9)
    up1, down1, up2, down2 = shift(eight, 1), shift(eight, -1), shift(first, 2), shift(second, -2)
    columns = columns.reshape(seq * here, local)
    x = lax.all_to_all(jnp.broadcast_to(columns[None], (heads,) + columns.shape), HD, 0, 0, tiled=True)
    own = (pack(eight, up1), pack(down1, up2, down2))
    other = [lax.ppermute(piece, "c", [(0, 1), (1, 0)]) for piece in own]
    where = jnp.stack([lax.axis_index("z"), lax.axis_index("xh"), lax.axis_index("c")]).astype(jnp.int32)
    mixed = column_part(where, x, norm_gain.reshape(1, -1), own, other)
    back = lax.all_to_all(mixed.reshape(seq, here, local), SEQ, 0, 0, tiled=True)
    return (stream_out[None], back.reshape(1, steps, local))


def solution(mesh):
    fine = Mesh(mesh.devices.reshape(16, 2, 2, 4, 2), SEQ + HD)
    rows = P(SEQ, None, HD)
    return jax.shard_map(
        on_device,
        mesh=fine,
        in_specs=(rows, rows, rows, rows, P(HD, None), P(), rows),
        out_specs=(rows, rows),
        check_vma=False,
    )
```

```python
import functools

import jax
import jax.numpy as jnp
from jax import lax
from jax.experimental import pallas as pl
from jax.experimental.pallas import tpu as pltpu
from jax.sharding import Mesh, PartitionSpec as P

HEAD = 128
EPS = 1e-05
NEG = -1e30
VMEM_BYTES = 60 * 1024 * 1024
SEQ = ("z", "xh", "c")
HD = ("y", "xl")


def softmax_mix(q, k, v, mask):
    s = lax.dot_general(q, k, (((1,), (1,)), ((), ())), preferred_element_type=jnp.float32)
    s = jnp.where(mask, s * (HEAD ** -0.5), NEG)
    p = jnp.exp(s - jnp.max(s, axis=-1, keepdims=True))
    w = (p / jnp.sum(p, axis=-1, keepdims=True)).astype(jnp.bfloat16)
    return jnp.dot(w, v, preferred_element_type=jnp.float32).astype(jnp.bfloat16)


def row_kernel(q_hbm, k_hbm, v_hbm, w_hbm, out_hbm, q_ref, k_ref, v_ref, w_ref, out_ref, sems, out_sems):
    copies = [
        pltpu.make_async_copy(src, dst, sems.at[i])
        for i, (src, dst) in enumerate(((q_hbm, q_ref), (k_hbm, k_ref), (v_hbm, v_ref), (w_hbm, w_ref)))
    ]
    for copy in copies:
        copy.start()
    for copy in copies[:3]:
        copy.wait()
    n = q_ref.shape[0]
    mask = lax.broadcasted_iota(jnp.int32, (n, n), 0) >= lax.broadcasted_iota(jnp.int32, (n, n), 1)
    mixed = []
    for h in range(q_ref.shape[1] // HEAD):
        cols = slice(h * HEAD, (h + 1) * HEAD)
        mixed.append(softmax_mix(q_ref[:, cols], k_ref[:, cols], v_ref[:, cols], mask))
    mixed = jnp.concatenate(mixed, axis=1)
    copies[3].wait()
    width = out_ref.shape[2]
    parts = []
    for part in range(out_ref.shape[0]):
        out_ref[part] = jnp.dot(
            mixed, w_ref[:, part * width : (part + 1) * width], preferred_element_type=jnp.float32
        ).astype(jnp.bfloat16)
        parts.append(pltpu.make_async_copy(out_ref.at[part], out_hbm.at[part], out_sems.at[part]))
        parts[-1].start()
    for copy in parts:
        copy.wait()


def row_part(q, k, v, w, heads):
    n, local = q.shape
    width = w.shape[1] // heads
    tile = pltpu.VMEM((n, local), jnp.bfloat16)
    return pl.pallas_call(
        row_kernel,
        out_shape=jax.ShapeDtypeStruct((heads, n, width), jnp.bfloat16),
        in_specs=[pl.BlockSpec(memory_space=pltpu.HBM)] * 4,
        out_specs=pl.BlockSpec(memory_space=pltpu.HBM),
        scratch_shapes=[
            tile,
            tile,
            tile,
            pltpu.VMEM(w.shape, jnp.bfloat16),
            pltpu.VMEM((heads, n, width), jnp.bfloat16),
            pltpu.SemaphoreType.DMA((4,)),
            pltpu.SemaphoreType.DMA((heads,)),
        ],
        compiler_params=pltpu.CompilerParams(vmem_limit_bytes=VMEM_BYTES),
        cost_estimate=pl.CostEstimate(
            flops=2 * n * local * (n * 2 + w.shape[1]), bytes_accessed=3 * 2**20, transcendentals=2 * n * n
        ),
        name="row_attention",
    )(q, k, v, w)


def pack_kernel(*refs):
    pieces, out_ref = refs[:-1], refs[-1]
    at = 0
    for ref in pieces:
        for i in range(ref.shape[0]):
            out_ref[at + i] = ref[i]
        at += ref.shape[0]


def pack(*pieces, weight=0):
    total = sum(p.shape[0] for p in pieces)
    shape = (total,) + pieces[0].shape[1:]
    size = 4
    for d in shape:
        size *= d
    vm = pl.BlockSpec(memory_space=pltpu.VMEM)
    return pl.pallas_call(
        pack_kernel,
        out_shape=jax.ShapeDtypeStruct(shape, pieces[0].dtype),
        in_specs=[vm] * len(pieces),
        out_specs=vm,
        compiler_params=pltpu.CompilerParams(vmem_limit_bytes=4 * 1024 * 1024),
        cost_estimate=pl.CostEstimate(flops=weight, bytes_accessed=size, transcendentals=0),
        name="pack",
    )(*pieces)


def group_kernel(pair_ref, up8_ref, down4_ref, up4_ref, event_ref, eight_ref, first_ref, second_ref):
    for i, ref in enumerate((pair_ref, up8_ref, down4_ref, up4_ref)):
        for o in (0, 1):
            eight_ref[2 * i + o] = ref[o]
    for o in (0, 1):
        first_ref[o] = pair_ref[o]
        first_ref[2 + o] = up4_ref[o]
        second_ref[o] = pair_ref[o]
        second_ref[2 + o] = down4_ref[o]


def group(pair, up8, down4, up4, event, weight):
    vm = pl.BlockSpec(memory_space=pltpu.VMEM)
    shape = pair.shape[1:]
    return pl.pallas_call(
        group_kernel,
        out_shape=[jax.ShapeDtypeStruct((n,) + shape, pair.dtype) for n in (8, 4, 4)],
        in_specs=[vm] * 5,
        out_specs=[vm] * 3,
        compiler_params=pltpu.CompilerParams(vmem_limit_bytes=4 * 1024 * 1024),
        cost_estimate=pl.CostEstimate(flops=weight, bytes_accessed=16 * pair.size, transcendentals=0),
        name="group",
    )(pair, up8, down4, up4, event)


FOUR = (0, 8, -4, 4)
EIGHT = [(f, o) for f in FOUR for o in (0, 1)]
SLOTS = (
    EIGHT
    + [(1 + f, o) for f, o in EIGHT]
    + [(-1 + f, o) for f, o in EIGHT]
    + [(2 + f, o) for f in (0, 4) for o in (0, 1)]
    + [(-2 + f, o) for f in (0, -4) for o in (0, 1)]
)


def column_kernel(count, where_ref, x_ref, gain_ref, *refs):
    own, other = refs[:count], refs[count : 2 * count]
    out_ref, w_ref, normed_ref, sems = refs[2 * count :]
    z, xh, core = where_ref[0], where_ref[1], where_ref[2]
    places = [
        (lax.rem(z + (off + 16), 16), 1 - xh if flip else xh) for off, flip in SLOTS
    ]
    copies = []
    for ref in other:
        for i in range(ref.shape[0]):
            zi, xi = places[len(copies)]
            copies.append(
                pltpu.make_async_copy(ref.at[i], w_ref.at[:, zi, xi, 1 - core], sems.at[len(copies)])
            )
            copies[-1].start()
    at = 0
    for ref in own:
        for i in range(ref.shape[0]):
            zi, xi = places[at]
            at += 1
            for j in range(3):
                w_ref[j, zi, xi, core] = ref[i, j]
    heads, n, local = x_ref.shape
    total = jnp.zeros((n, 1), jnp.float32)
    for h in range(heads):
        x = x_ref[h].astype(jnp.float32)
        total = total + jnp.sum(x * x, axis=1, keepdims=True)
    scale = lax.rsqrt(total / (heads * local) + EPS)
    for h in range(heads):
        cols = slice(h * local, (h + 1) * local)
        normed_ref[:, cols] = (x_ref[h].astype(jnp.float32) * scale * gain_ref[:, cols]).astype(jnp.bfloat16)
    for copy in copies:
        copy.wait()
    parts = []
    for j in range(3):
        w = w_ref[j].reshape(heads * local, local)
        parts.append(
            jnp.dot(normed_ref[...], w, preferred_element_type=jnp.float32).astype(jnp.bfloat16)
        )
    q, k, v = parts
    t0 = lax.broadcasted_iota(jnp.int32, (n, n), 0)
    t1 = lax.broadcasted_iota(jnp.int32, (n, n), 1)
    cols_here = 4
    mask = (t0 >= t1) & ((t0 & (cols_here - 1)) == (t1 & (cols_here - 1)))
    for h in range(local // HEAD):
        cols = slice(h * HEAD, (h + 1) * HEAD)
        out_ref[:, cols] = softmax_mix(q[:, cols], k[:, cols], v[:, cols], mask)


def column_part(where, x, gain, own, other):
    count = len(own)
    heads, n, local = x.shape
    rows = own[0].shape[2]
    vm = pl.BlockSpec(memory_space=pltpu.VMEM)
    return pl.pallas_call(
        functools.partial(column_kernel, count),
        out_shape=jax.ShapeDtypeStruct((n, local), jnp.bfloat16),
        in_specs=[pl.BlockSpec(memory_space=pltpu.SMEM)] + [vm] * (2 + count) + [pl.BlockSpec(memory_space=pl.ANY)] * count,
        out_specs=vm,
        scratch_shapes=[
            pltpu.VMEM((3, 16, 2, 2, rows, local), jnp.bfloat16),
            pltpu.VMEM((n, heads * local), jnp.bfloat16),
            pltpu.SemaphoreType.DMA((len(SLOTS),)),
        ],
        compiler_params=pltpu.CompilerParams(vmem_limit_bytes=20 * 1024 * 1024),
        cost_estimate=pl.CostEstimate(
            flops=2 * n * heads * local * 3 * local, bytes_accessed=5 * 2**20, transcendentals=2 * n * n
        ),
        name="column_attention",
    )(where, x, gain, *own, *other)


def shift(x, d):
    return lax.ppermute(x, "z", [((i + d) % 16, i) for i in range(16)])


def on_device(stream_in, row_query, row_key, row_value, out_weight, norm_gain, qkv_weight):
    _, steps, local = row_query.shape
    heads = norm_gain.shape[0] // local
    seq = 64
    here = steps // seq

    w = jnp.transpose(qkv_weight, (1, 0, 2))[None]
    theirs = lax.ppermute(w, "xh", [(0, 1), (1, 0)])
    partial = row_part(row_query[0], row_key[0], row_value[0], out_weight, heads)
    pair = pack(w, theirs, weight=10**10)
    parts = lax.all_to_all(partial, HD, 0, 0, tiled=True)
    up8, down4, up4 = shift(pair, 8), shift(pair, -4), shift(pair, 4)
    stream = stream_in[0].astype(jnp.float32) + jnp.sum(parts.astype(jnp.float32), axis=0)
    stream_out = stream.astype(jnp.bfloat16)
    columns = lax.all_to_all(stream_out.reshape(seq, here, local), SEQ, 0, 0, tiled=True)
    eight, first, second = group(pair, up8, down4, up4, stream_out, 10**9)
    up1, down1, up2, down2 = shift(eight, 1), shift(eight, -1), shift(first, 2), shift(second, -2)
    columns = columns.reshape(seq * here, local)
    x = lax.all_to_all(jnp.broadcast_to(columns[None], (heads,) + columns.shape), HD, 0, 0, tiled=True)
    own = (pack(eight, up1), pack(down1, up2, down2))
    other = [lax.ppermute(piece, "c", [(0, 1), (1, 0)]) for piece in own]
    where = jnp.stack([lax.axis_index("z"), lax.axis_index("xh"), lax.axis_index("c")]).astype(jnp.int32)
    mixed = column_part(where, x, norm_gain.reshape(1, -1), own, other)
    back = lax.all_to_all(mixed.reshape(seq, here, local), SEQ, 0, 0, tiled=True)
    return (stream_out[None], back.reshape(1, steps, local))


def solution(mesh):
    fine = Mesh(mesh.devices.reshape(16, 2, 2, 4, 2), SEQ + HD)
    rows = P(SEQ, None, HD)
    return jax.shard_map(
        on_device,
        mesh=fine,
        in_specs=(rows, rows, rows, rows, P(HD, None), P(), rows),
        out_specs=(rows, rows),
        check_vma=False,
    )
```

```python
import functools

import jax
import jax.numpy as jnp
from jax import lax
from jax.experimental import pallas as pl
from jax.experimental.pallas import tpu as pltpu
from jax.sharding import Mesh, PartitionSpec as P

HEAD = 128
EPS = 1e-05
NEG = -1e30
VMEM_BYTES = 60 * 1024 * 1024
SEQ = ("z", "xh", "c")
HD = ("y", "xl")
TURN = 32


def softmax_mix(q, k, v, mask):
    s = lax.dot_general(q, k, (((1,), (1,)), ((), ())), preferred_element_type=jnp.float32)
    s = jnp.where(mask, s * (HEAD ** -0.5), NEG)
    p = jnp.exp(s - jnp.max(s, axis=-1, keepdims=True))
    w = (p / jnp.sum(p, axis=-1, keepdims=True)).astype(jnp.bfloat16)
    return jnp.dot(w, v, preferred_element_type=jnp.float32)


def row_kernel(q_hbm, k_hbm, v_hbm, w_hbm, out_hbm, q_ref, k_ref, v_ref, w_ref, out_ref, sems, out_sems):
    copies = [
        pltpu.make_async_copy(src, dst, sems.at[i])
        for i, (src, dst) in enumerate(((q_hbm, q_ref), (k_hbm, k_ref), (v_hbm, v_ref), (w_hbm, w_ref)))
    ]
    for copy in copies:
        copy.start()
    for copy in copies[:3]:
        copy.wait()
    n = q_ref.shape[0]
    mask = lax.broadcasted_iota(jnp.int32, (n, n), 0) >= lax.broadcasted_iota(jnp.int32, (n, n), 1)
    mixed = []
    for h in range(q_ref.shape[1] // HEAD):
        cols = slice(h * HEAD, (h + 1) * HEAD)
        mixed.append(softmax_mix(q_ref[:, cols], k_ref[:, cols], v_ref[:, cols], mask).astype(jnp.bfloat16))
    mixed = jnp.concatenate(mixed, axis=1)
    copies[3].wait()
    width = out_ref.shape[2]
    parts = []
    for part in range(out_ref.shape[0]):
        out_ref[part] = jnp.dot(
            mixed, w_ref[:, part * width : (part + 1) * width], preferred_element_type=jnp.float32
        ).astype(jnp.bfloat16)
        parts.append(pltpu.make_async_copy(out_ref.at[part], out_hbm.at[part], out_sems.at[part]))
        parts[-1].start()
    for copy in parts:
        copy.wait()


def row_part(q, k, v, w, heads):
    n, local = q.shape
    width = w.shape[1] // heads
    tile = pltpu.VMEM((n, local), jnp.bfloat16)
    return pl.pallas_call(
        row_kernel,
        out_shape=jax.ShapeDtypeStruct((heads, n, width), jnp.bfloat16),
        in_specs=[pl.BlockSpec(memory_space=pltpu.HBM)] * 4,
        out_specs=pl.BlockSpec(memory_space=pltpu.HBM),
        scratch_shapes=[
            tile,
            tile,
            tile,
            pltpu.VMEM(w.shape, jnp.bfloat16),
            pltpu.VMEM((heads, n, width), jnp.bfloat16),
            pltpu.SemaphoreType.DMA((4,)),
            pltpu.SemaphoreType.DMA((heads,)),
        ],
        compiler_params=pltpu.CompilerParams(vmem_limit_bytes=VMEM_BYTES),
        cost_estimate=pl.CostEstimate(
            flops=2 * n * local * (n * 2 + w.shape[1]), bytes_accessed=3 * 2**20, transcendentals=2 * n * n
        ),
        name="row_attention",
    )(q, k, v, w)


def pack_kernel(*refs):
    pieces, out_ref = refs[:-1], refs[-1]
    at = 0
    for ref in pieces:
        for i in range(ref.shape[0]):
            out_ref[at + i] = ref[i]
        at += ref.shape[0]


def pack(*pieces, weight=0):
    total = sum(p.shape[0] for p in pieces)
    shape = (total,) + pieces[0].shape[1:]
    size = 4
    for d in shape:
        size *= d
    vm = pl.BlockSpec(memory_space=pltpu.VMEM)
    return pl.pallas_call(
        pack_kernel,
        out_shape=jax.ShapeDtypeStruct(shape, pieces[0].dtype),
        in_specs=[vm] * len(pieces),
        out_specs=vm,
        compiler_params=pltpu.CompilerParams(vmem_limit_bytes=4 * 1024 * 1024),
        cost_estimate=pl.CostEstimate(flops=weight, bytes_accessed=size, transcendentals=0),
        name="pack",
    )(*pieces)


def group_kernel(pair_ref, up8_ref, down4_ref, up4_ref, event_ref, eight_ref, first_ref, second_ref):
    for i, ref in enumerate((pair_ref, up8_ref, down4_ref, up4_ref)):
        for o in (0, 1):
            eight_ref[2 * i + o] = ref[o]
    for o in (0, 1):
        first_ref[o] = pair_ref[o]
        first_ref[2 + o] = up4_ref[o]
        second_ref[o] = pair_ref[o]
        second_ref[2 + o] = down4_ref[o]


def group(pair, up8, down4, up4, event, weight):
    vm = pl.BlockSpec(memory_space=pltpu.VMEM)
    shape = pair.shape[1:]
    return pl.pallas_call(
        group_kernel,
        out_shape=[jax.ShapeDtypeStruct((n,) + shape, pair.dtype) for n in (8, 4, 4)],
        in_specs=[vm] * 5,
        out_specs=[vm] * 3,
        compiler_params=pltpu.CompilerParams(vmem_limit_bytes=4 * 1024 * 1024),
        cost_estimate=pl.CostEstimate(flops=weight, bytes_accessed=16 * pair.size, transcendentals=0),
        name="group",
    )(pair, up8, down4, up4, event)


FOUR = (0, 8, -4, 4)
EIGHT = [(f, o) for f in FOUR for o in (0, 1)]
SLOTS = (
    EIGHT
    + [(1 + f, o) for f, o in EIGHT]
    + [(-1 + f, o) for f, o in EIGHT]
    + [(2 + f, o) for f in (0, 4) for o in (0, 1)]
    + [(-2 + f, o) for f in (0, -4) for o in (0, 1)]
)


def column_kernel(count, where_ref, x_ref, gain_ref, *refs):
    pieces, (out_ref, w_ref, normed_ref) = refs[: 2 * count], refs[2 * count :]
    z, xh, core = where_ref[0], where_ref[1], where_ref[2]
    for side in (0, 1):
        c = core if side == 0 else 1 - core
        slots = iter(SLOTS)
        for ref in pieces[side * count : (side + 1) * count]:
            for i in range(ref.shape[0]):
                off, flip = next(slots)
                zi = lax.rem(z + (off + 16), 16)
                xi = 1 - xh if flip else xh
                for j in range(3):
                    w_ref[j, zi, xi, c] = ref[i, j]
    heads, n, local = x_ref.shape
    total = jnp.zeros((n, 1), jnp.float32)
    for h in range(heads):
        x = x_ref[h].astype(jnp.float32)
        total = total + jnp.sum(x * x, axis=1, keepdims=True)
    scale = lax.rsqrt(total / (heads * local) + EPS)
    for h in range(heads):
        cols = slice(h * local, (h + 1) * local)
        normed_ref[:, cols] = (x_ref[h].astype(jnp.float32) * scale * gain_ref[:, cols]).astype(jnp.bfloat16)
    parts = []
    for j in range(3):
        w = w_ref[j].reshape(heads * local, local)
        parts.append(
            jnp.dot(normed_ref[...], w, preferred_element_type=jnp.float32).astype(jnp.bfloat16)
        )
    q, k, v = parts
    t0 = lax.broadcasted_iota(jnp.int32, (n, n), 0)
    t1 = lax.broadcasted_iota(jnp.int32, (n, n), 1)
    cols_here = 4
    mask = (t0 >= t1) & ((t0 & (cols_here - 1)) == (t1 & (cols_here - 1)))
    mixed = []
    for h in range(local // HEAD):
        cols = slice(h * HEAD, (h + 1) * HEAD)
        one = softmax_mix(q[:, cols], k[:, cols], v[:, cols], mask)
        mixed.append(one.reshape(n // cols_here, cols_here, HEAD))
    mixed = jnp.concatenate(mixed, axis=1).astype(jnp.bfloat16)
    rows = mixed.shape[0]
    out_ref[: rows - TURN] = mixed[TURN:]
    out_ref[rows - TURN :] = mixed[:TURN]


def column_part(where, x, gain, own, other):
    count = len(own)
    heads, n, local = x.shape
    rows = own[0].shape[2]
    vm = pl.BlockSpec(memory_space=pltpu.VMEM)
    return pl.pallas_call(
        functools.partial(column_kernel, count),
        out_shape=jax.ShapeDtypeStruct((n // 4, 4 * local // HEAD, HEAD), jnp.bfloat16),
        in_specs=[pl.BlockSpec(memory_space=pltpu.SMEM)] + [vm] * (2 + 2 * count),
        out_specs=vm,
        scratch_shapes=[
            pltpu.VMEM((3, 16, 2, 2, rows, local), jnp.bfloat16),
            pltpu.VMEM((n, heads * local), jnp.bfloat16),
        ],
        compiler_params=pltpu.CompilerParams(vmem_limit_bytes=20 * 1024 * 1024),
        cost_estimate=pl.CostEstimate(
            flops=2 * n * heads * local * 3 * local, bytes_accessed=5 * 2**20, transcendentals=2 * n * n
        ),
        name="column_attention",
    )(where, x, gain, *own, *other)


def shift(x, d):
    return lax.ppermute(x, "z", [((i + d) % 16, i) for i in range(16)])


def on_device(stream_in, row_query, row_key, row_value, out_weight, norm_gain, qkv_weight):
    _, steps, local = row_query.shape
    heads = norm_gain.shape[0] // local
    seq = 64
    here = steps // seq

    w = jnp.transpose(qkv_weight, (1, 0, 2))[None]
    theirs = lax.ppermute(w, "xh", [(0, 1), (1, 0)])
    partial = row_part(row_query[0], row_key[0], row_value[0], out_weight, heads)
    pair = pack(w, theirs, weight=10**10)
    parts = lax.all_to_all(partial, HD, 0, 0, tiled=True)
    up8, down4, up4 = shift(pair, 8), shift(pair, -4), shift(pair, 4)
    stream = stream_in[0].astype(jnp.float32) + jnp.sum(parts.astype(jnp.float32), axis=0)
    stream_out = stream.astype(jnp.bfloat16)
    columns = lax.all_to_all(stream_out.reshape(seq, here, local), SEQ, 0, 0, tiled=True)
    eight, first, second = group(pair, up8, down4, up4, stream_out, 10**9)
    up1, down1, up2, down2 = shift(eight, 1), shift(eight, -1), shift(first, 2), shift(second, -2)
    columns = columns.reshape(seq * here, local)
    x = lax.all_to_all(jnp.broadcast_to(columns[None], (heads,) + columns.shape), HD, 0, 0, tiled=True)
    own = (pack(eight, up1), pack(down1, weight=3000000000), pack(up2, down2, weight=1000000000))
    other = [lax.ppermute(piece, "c", [(0, 1), (1, 0)]) for piece in own]
    where = jnp.stack([lax.axis_index("z"), lax.axis_index("xh"), lax.axis_index("c")]).astype(jnp.int32)
    mixed = column_part(where, x, norm_gain.reshape(1, -1), own, other)
    turned = [[(i + TURN) % seq for i in range(seq)]]
    back = lax.all_to_all(mixed, SEQ, 0, 0, tiled=True, axis_index_groups=turned)
    back = jnp.concatenate([back[seq - TURN :], back[: seq - TURN]], axis=0)
    back = back.reshape(seq, local // HEAD, here, HEAD).transpose(0, 2, 1, 3)
    return (stream_out[None], back.reshape(1, steps, local))


def solution(mesh):
    fine = Mesh(mesh.devices.reshape(16, 2, 2, 4, 2), SEQ + HD)
    rows = P(SEQ, None, HD)
    return jax.shard_map(
        on_device,
        mesh=fine,
        in_specs=(rows, rows, rows, rows, P(HD, None), P(), rows),
        out_specs=(rows, rows),
        check_vma=False,
    )
```

```python
import functools

import jax
import jax.numpy as jnp
from jax import lax
from jax.experimental import pallas as pl
from jax.experimental.pallas import tpu as pltpu
from jax.sharding import Mesh, PartitionSpec as P

HEAD = 128
EPS = 1e-05
NEG = -1e30
VMEM_BYTES = 60 * 1024 * 1024
SEQ = ("z", "xh", "c")
HD = ("y", "xl")
TURN = 32
FIRST = 16


def softmax_mix(q, k, v, mask):
    s = lax.dot_general(q, k, (((1,), (1,)), ((), ())), preferred_element_type=jnp.float32)
    s = jnp.where(mask, s * (HEAD ** -0.5), NEG)
    p = jnp.exp(s - jnp.max(s, axis=-1, keepdims=True))
    w = (p / jnp.sum(p, axis=-1, keepdims=True)).astype(jnp.bfloat16)
    return jnp.dot(w, v, preferred_element_type=jnp.float32)


def row_kernel(q_hbm, k_hbm, v_hbm, w_hbm, out_hbm, q_ref, k_ref, v_ref, w_ref, out_ref, sems, out_sems):
    copies = [
        pltpu.make_async_copy(src, dst, sems.at[i])
        for i, (src, dst) in enumerate(((q_hbm, q_ref), (k_hbm, k_ref), (v_hbm, v_ref), (w_hbm, w_ref)))
    ]
    for copy in copies:
        copy.start()
    for copy in copies[:3]:
        copy.wait()
    n = q_ref.shape[0]
    mask = lax.broadcasted_iota(jnp.int32, (n, n), 0) >= lax.broadcasted_iota(jnp.int32, (n, n), 1)
    mixed = []
    for h in range(q_ref.shape[1] // HEAD):
        cols = slice(h * HEAD, (h + 1) * HEAD)
        mixed.append(softmax_mix(q_ref[:, cols], k_ref[:, cols], v_ref[:, cols], mask).astype(jnp.bfloat16))
    mixed = jnp.concatenate(mixed, axis=1)
    copies[3].wait()
    width = out_ref.shape[2]
    parts = []
    for part in range(out_ref.shape[0]):
        out_ref[part] = jnp.dot(
            mixed, w_ref[:, part * width : (part + 1) * width], preferred_element_type=jnp.float32
        ).astype(jnp.bfloat16)
        parts.append(pltpu.make_async_copy(out_ref.at[part], out_hbm.at[part], out_sems.at[part]))
        parts[-1].start()
    for copy in parts:
        copy.wait()


def row_part(q, k, v, w, heads):
    n, local = q.shape
    width = w.shape[1] // heads
    tile = pltpu.VMEM((n, local), jnp.bfloat16)
    return pl.pallas_call(
        row_kernel,
        out_shape=jax.ShapeDtypeStruct((heads, n, width), jnp.bfloat16),
        in_specs=[pl.BlockSpec(memory_space=pltpu.HBM)] * 4,
        out_specs=pl.BlockSpec(memory_space=pltpu.HBM),
        scratch_shapes=[
            tile,
            tile,
            tile,
            pltpu.VMEM(w.shape, jnp.bfloat16),
            pltpu.VMEM((heads, n, width), jnp.bfloat16),
            pltpu.SemaphoreType.DMA((4,)),
            pltpu.SemaphoreType.DMA((heads,)),
        ],
        compiler_params=pltpu.CompilerParams(vmem_limit_bytes=VMEM_BYTES),
        cost_estimate=pl.CostEstimate(
            flops=2 * n * local * (n * 2 + w.shape[1]), bytes_accessed=3 * 2**20, transcendentals=2 * n * n
        ),
        name="row_attention",
    )(q, k, v, w)


def pack_kernel(*refs):
    pieces, out_ref = refs[:-1], refs[-1]
    at = 0
    for ref in pieces:
        for i in range(ref.shape[0]):
            out_ref[at + i] = ref[i]
        at += ref.shape[0]


def pack(*pieces, weight=0):
    total = sum(p.shape[0] for p in pieces)
    shape = (total,) + pieces[0].shape[1:]
    size = 4
    for d in shape:
        size *= d
    vm = pl.BlockSpec(memory_space=pltpu.VMEM)
    return pl.pallas_call(
        pack_kernel,
        out_shape=jax.ShapeDtypeStruct(shape, pieces[0].dtype),
        in_specs=[vm] * len(pieces),
        out_specs=vm,
        compiler_params=pltpu.CompilerParams(vmem_limit_bytes=4 * 1024 * 1024),
        cost_estimate=pl.CostEstimate(flops=weight, bytes_accessed=size, transcendentals=0),
        name="pack",
    )(*pieces)


def group_kernel(pair_ref, up8_ref, down4_ref, up4_ref, event_ref, eight_ref, first_ref, second_ref):
    for i, ref in enumerate((pair_ref, up8_ref, down4_ref, up4_ref)):
        for o in (0, 1):
            eight_ref[2 * i + o] = ref[o]
    for o in (0, 1):
        first_ref[o] = pair_ref[o]
        first_ref[2 + o] = up4_ref[o]
        second_ref[o] = pair_ref[o]
        second_ref[2 + o] = down4_ref[o]


def group(pair, up8, down4, up4, event, weight):
    vm = pl.BlockSpec(memory_space=pltpu.VMEM)
    shape = pair.shape[1:]
    return pl.pallas_call(
        group_kernel,
        out_shape=[jax.ShapeDtypeStruct((n,) + shape, pair.dtype) for n in (8, 4, 4)],
        in_specs=[vm] * 5,
        out_specs=[vm] * 3,
        compiler_params=pltpu.CompilerParams(vmem_limit_bytes=4 * 1024 * 1024),
        cost_estimate=pl.CostEstimate(flops=weight, bytes_accessed=16 * pair.size, transcendentals=0),
        name="group",
    )(pair, up8, down4, up4, event)


FOUR = (0, 8, -4, 4)
EIGHT = [(f, o) for f in FOUR for o in (0, 1)]
SLOTS = (
    EIGHT
    + [(1 + f, o) for f, o in EIGHT]
    + [(-1 + f, o) for f, o in EIGHT]
    + [(2 + f, o) for f in (0, 4) for o in (0, 1)]
    + [(-2 + f, o) for f in (0, -4) for o in (0, 1)]
)


def column_kernel(count, where_ref, x_ref, gain_ref, *refs):
    pieces, (out_ref, w_ref, normed_ref) = refs[: 2 * count], refs[2 * count :]
    z, xh, core = where_ref[0], where_ref[1], where_ref[2]
    for side in (0, 1):
        c = core if side == 0 else 1 - core
        slots = iter(SLOTS)
        for ref in pieces[side * count : (side + 1) * count]:
            for i in range(ref.shape[0]):
                off, flip = next(slots)
                zi = lax.rem(z + (off + 16), 16)
                xi = 1 - xh if flip else xh
                for j in range(3):
                    w_ref[j, zi, xi, c] = ref[i, j]
    heads, n, local = x_ref.shape
    total = jnp.zeros((n, 1), jnp.float32)
    for h in range(heads):
        x = x_ref[h].astype(jnp.float32)
        total = total + jnp.sum(x * x, axis=1, keepdims=True)
    scale = lax.rsqrt(total / (heads * local) + EPS)
    for h in range(heads):
        cols = slice(h * local, (h + 1) * local)
        normed_ref[:, cols] = (x_ref[h].astype(jnp.float32) * scale * gain_ref[:, cols]).astype(jnp.bfloat16)
    parts = []
    for j in range(3):
        w = w_ref[j].reshape(heads * local, local)
        parts.append(
            jnp.dot(normed_ref[...], w, preferred_element_type=jnp.float32).astype(jnp.bfloat16)
        )
    q, k, v = parts
    t0 = lax.broadcasted_iota(jnp.int32, (n, n), 0)
    t1 = lax.broadcasted_iota(jnp.int32, (n, n), 1)
    cols_here = 4
    shift_by = cols_here * FIRST
    t0, t1 = (t0 + shift_by) & (n - 1), (t1 + shift_by) & (n - 1)
    mask = (t0 >= t1) & ((t0 & (cols_here - 1)) == (t1 & (cols_here - 1)))
    mixed = []
    for h in range(local // HEAD):
        cols = slice(h * HEAD, (h + 1) * HEAD)
        one = softmax_mix(q[:, cols], k[:, cols], v[:, cols], mask)
        mixed.append(one.reshape(n // cols_here, cols_here, HEAD))
    mixed = jnp.concatenate(mixed, axis=1).astype(jnp.bfloat16)
    rows = mixed.shape[0]
    turn = (TURN - FIRST) % rows
    if turn:
        out_ref[: rows - turn] = mixed[turn:]
        out_ref[rows - turn :] = mixed[:turn]
    else:
        out_ref[...] = mixed


def column_part(where, x, gain, own, other):
    count = len(own)
    heads, n, local = x.shape
    rows = own[0].shape[2]
    vm = pl.BlockSpec(memory_space=pltpu.VMEM)
    return pl.pallas_call(
        functools.partial(column_kernel, count),
        out_shape=jax.ShapeDtypeStruct((n // 4, 4 * local // HEAD, HEAD), jnp.bfloat16),
        in_specs=[pl.BlockSpec(memory_space=pltpu.SMEM)] + [vm] * (2 + 2 * count),
        out_specs=vm,
        scratch_shapes=[
            pltpu.VMEM((3, 16, 2, 2, rows, local), jnp.bfloat16),
            pltpu.VMEM((n, heads * local), jnp.bfloat16),
        ],
        compiler_params=pltpu.CompilerParams(vmem_limit_bytes=20 * 1024 * 1024),
        cost_estimate=pl.CostEstimate(
            flops=2 * n * heads * local * 3 * local, bytes_accessed=5 * 2**20, transcendentals=2 * n * n
        ),
        name="column_attention",
    )(where, x, gain, *own, *other)


def shift(x, d):
    return lax.ppermute(x, "z", [((i + d) % 16, i) for i in range(16)])


def on_device(stream_in, row_query, row_key, row_value, out_weight, norm_gain, qkv_weight):
    _, steps, local = row_query.shape
    heads = norm_gain.shape[0] // local
    seq = 64
    here = steps // seq

    w = jnp.transpose(qkv_weight, (1, 0, 2))[None]
    theirs = lax.ppermute(w, "xh", [(0, 1), (1, 0)])
    partial = row_part(row_query[0], row_key[0], row_value[0], out_weight, heads)
    pair = pack(w, theirs, weight=10**11)
    parts = lax.all_to_all(partial, HD, 0, 0, tiled=True)
    up8, down4, up4 = shift(pair, 8), shift(pair, -4), shift(pair, 4)
    stream = stream_in[0].astype(jnp.float32) + jnp.sum(parts.astype(jnp.float32), axis=0)
    stream_out = stream.astype(jnp.bfloat16)
    blocks = stream_out.reshape(seq, here, local)
    blocks = jnp.concatenate([blocks[FIRST:], blocks[:FIRST]], axis=0)
    turned = [[(i + FIRST) % seq for i in range(seq)]]
    columns = lax.all_to_all(blocks, SEQ, 0, 0, tiled=True, axis_index_groups=turned)
    eight, first, second = group(pair, up8, down4, up4, stream_out, 10**10)
    up1, down1, up2, down2 = shift(eight, 1), shift(eight, -1), shift(first, 2), shift(second, -2)
    columns = columns.reshape(seq * here, local)
    x = lax.all_to_all(jnp.broadcast_to(columns[None], (heads,) + columns.shape), HD, 0, 0, tiled=True)
    own = (pack(eight, up1), pack(down1, weight=3000000000), pack(up2, down2, weight=1000000000))
    other = [lax.ppermute(piece, "c", [(0, 1), (1, 0)]) for piece in own]
    where = jnp.stack([lax.axis_index("z"), lax.axis_index("xh"), lax.axis_index("c")]).astype(jnp.int32)
    mixed = column_part(where, x, norm_gain.reshape(1, -1), own, other)
    turned = [[(i + TURN) % seq for i in range(seq)]]
    back = lax.all_to_all(mixed, SEQ, 0, 0, tiled=True, axis_index_groups=turned)
    back = jnp.concatenate([back[seq - TURN :], back[: seq - TURN]], axis=0)
    back = back.reshape(seq, local // HEAD, here, HEAD).transpose(0, 2, 1, 3)
    return (stream_out[None], back.reshape(1, steps, local))


def solution(mesh):
    fine = Mesh(mesh.devices.reshape(16, 2, 2, 4, 2), SEQ + HD)
    rows = P(SEQ, None, HD)
    return jax.shard_map(
        on_device,
        mesh=fine,
        in_specs=(rows, rows, rows, rows, P(HD, None), P(), rows),
        out_specs=(rows, rows),
        check_vma=False,
    )
```
